512 devices in a mesh: mem: 32 (over x, y, z_hi), tile: 16 (over z_lo, core).
Axes of the slice: x: 4, y: 4, z: 16 (z_hi: 2, z_lo: 8; z = z_hi * 8 + z_lo), core: 2. Of those that a mesh axis runs over, the one named last changes fastest.
Arguments:
- starting_ensemble: bfloat16 [64, 8, 128, 1120], P('mem', None, 'tile'), may hold values from -6 to 6
- patch_lifting: bfloat16 [1120, 768], P('mem'), may hold values from -0.1875 to 0.1875
- query_keyvalue_lift: bfloat16 [768, 2304], P(None, 'mem'), may hold values from -0.21875 to 0.21875
- output_combiner: bfloat16 [768, 768], P(None, 'mem'), may hold values from -0.21875 to 0.21875
- decoder_linear_map: bfloat16 [768, 1120], P(None, 'mem'), may hold values from -0.21875 to 0.21875
- cosine_logit_scale: float32 [12], replicated, may hold values from 2 to 30
- sensor_variable_loadings: bfloat16 [16, 70], replicated, may hold values from -0.75 to 0.75
- sensor_gridpoint: int32 [32, 16, 256], P('mem', 'tile'), may hold values from 0 to 31, as said below
- sensor_domain_index: int32 [32, 16, 256], P('mem', 'tile'), may hold values from 0 to 1, as said below
- sensor_channel_list: int32 [32, 16, 256], P('mem', 'tile'), may hold values from 0 to 15
- sensor_reading: float32 [32, 16, 256], P('mem', 'tile'), may hold values from -6 to 6
- sensor_noise_deviation: float32 [32, 16, 256], P('mem', 'tile'), may hold values from 0.5 to 2
Outputs:
- analysis: bfloat16 [64, 8, 128, 1120], P('mem', None, 'tile')
The draws below stay inside these ranges and needn't reach their ends.
Inputs may be any that keep to these rules, and one draw needn't show every extreme that they name: `sensor_gridpoint`: a point of the piece's 2 tokens. `sensor_domain_index`: differs by at most one from sensor_gridpoint // 16 of the same observation.
All inputs are finite; a program needn't handle non-finite values. Where the reference program divides by a largest or mean magnitude, that divisor is 1e-20 or more.
Results may differ from the reference program's by a relative error of at most 0.039.
Values may be sent and summed in bfloat16 or wider, within the bound.
No kernel may reach another device: no remote copies, remote signals or barrier semaphores. Data moves between devices by JAX's collectives and lax.ppermute only.
A program may use at most 64 MiB of HBM per device.

```python
import math
import jax
import jax.numpy as jnp
from jax import lax

VARS = 70
PATCH = 16
FEAT = 1120
FOCUS_COUNT = 12
D = 768
PANE_SIDE = 8
ENS = 64
LAT = 8
LON_DEV = 8
LON = 128
TOKP = 2
OBS_DEV = 256
NCH = 16
NS_ITERS = 5
N_MEM = 32
N_TILE = 16


def obs_places(key):
    return jax.random.randint(key, (N_MEM, N_TILE, OBS_DEV), 0, TOKP * PATCH)


def draw_sensor_gridpoint(key, part):
    places = obs_places(key)
    return places.astype(jnp.int32)


def draw_sensor_domain_index(key, part):
    places = obs_places(key)
    key = jax.random.fold_in(key, 7)
    offset = jax.random.randint(key, places.shape, -1, 2)
    return jnp.clip(places // PATCH + offset, 0, TOKP - 1).astype(jnp.int32)


def place_ends(entries, stream_key, smallest, high):
    place = [jax.random.randint(jax.random.fold_in(stream_key, axis), (), 0, length) for axis, length in enumerate(entries.shape)]
    main_axis = entries.shape.index(max(entries.shape))
    next_to = place[:main_axis] + [(place[main_axis] + 1) % entries.shape[main_axis]] + place[main_axis + 1:]
    return entries.at[tuple(place)].set(smallest).at[tuple(next_to)].set(high)


def levels(key, shape, shards, least, top_value):
    loudness = 1.0
    for dim, parts in shards:
        steps = jax.random.uniform(jax.random.fold_in(jax.random.fold_in(key, 6), dim), (parts,), jnp.float32, least / len(shards), top_value / len(shards))
        loudness = loudness * jnp.repeat(jnp.exp(steps), shape[dim] // parts).reshape((-1,) + (1,) * (len(shape) - 1 - dim))
    return loudness


def centred(rng, extent, scale, most, cuts=(), kind=jnp.bfloat16):
    loudness = levels(rng, extent, cuts, -0.22, 0.18) if cuts else 1.0
    values = jax.random.normal(rng, extent, jnp.float32) * scale * loudness
    return jnp.minimum(jnp.maximum(values, -most), most).astype(kind)


def setup_inputs(seed: int = 0) -> dict:
    streams_of = jax.random.split(jax.random.key(seed), 13)
    starting_ensemble = centred(streams_of[0], (ENS, LAT, LON, FEAT), 1.0, 6.0, ((0, 32), (2, 16)))
    patch_lifting = centred(streams_of[1], (FEAT, D), FEAT ** -0.5, 0.1875, ((0, 32),))
    query_keyvalue_lift = centred(streams_of[2], (D, 3 * D), D ** -0.5, 0.21875, ((1, 32),))
    output_combiner = centred(streams_of[3], (D, D), D ** -0.5, 0.21875, ((1, 32),))
    decoder_linear_map = centred(streams_of[4], (D, FEAT), D ** -0.5, 0.21875, ((1, 32),))
    cosine_logit_scale = jnp.clip(jnp.exp(jax.random.uniform(streams_of[5], (FOCUS_COUNT,), jnp.float32, math.log(2.0), math.log(30.0))), 2.0, 30.0)
    sensor_variable_loadings = centred(streams_of[6], (NCH, VARS), VARS ** -0.5, 0.75)
    sensor_gridpoint = draw_sensor_gridpoint(jax.random.fold_in(streams_of[12], 71), 0)
    sensor_domain_index = draw_sensor_domain_index(jax.random.fold_in(streams_of[12], 71), 0)
    sensor_channel_list = place_ends(jax.random.randint(streams_of[9], (N_MEM, N_TILE, OBS_DEV), 0, NCH), jax.random.fold_in(streams_of[9], 1), 0, NCH - 1).astype(jnp.int32)
    sensor_reading = centred(streams_of[10], (N_MEM, N_TILE, OBS_DEV), 1.0, 6.0, ((0, 32), (1, 16)), jnp.float32)
    sensor_noise_deviation = jnp.clip(jnp.exp(math.log(2.0) - 1.3862944 * jax.random.uniform(streams_of[11], (N_MEM, N_TILE, OBS_DEV), jnp.float32) ** levels(streams_of[11], (N_MEM, N_TILE, OBS_DEV), ((0, 32), (1, 16)), -0.2, 0.2)), 0.5, 2.0)
    return {"starting_ensemble": starting_ensemble, "patch_lifting": patch_lifting, "query_keyvalue_lift": query_keyvalue_lift, "output_combiner": output_combiner, "decoder_linear_map": decoder_linear_map, "cosine_logit_scale": cosine_logit_scale, "sensor_variable_loadings": sensor_variable_loadings, "sensor_gridpoint": sensor_gridpoint, "sensor_domain_index": sensor_domain_index, "sensor_channel_list": sensor_channel_list, "sensor_reading": sensor_reading, "sensor_noise_deviation": sensor_noise_deviation}


eps_norm = 1e-05
normalizing_guard = 1e-06

def layer_norm(values):
    values = values.astype(jnp.float32)
    center = values - lax.optimization_barrier(jnp.mean(values, axis=-1, keepdims=True))
    spread = lax.optimization_barrier(jnp.mean(center * center, axis=-1, keepdims=True))
    return center * lax.rsqrt(spread + eps_norm)

def unit_rows(values):
    values = values.astype(jnp.float32)
    return (values * lax.rsqrt(lax.optimization_barrier(jnp.sum(values * values, axis=-1, keepdims=True)) + normalizing_guard)).astype(jnp.bfloat16)

def pane_cosine_mixer(padded_part, query_keyvalue_lift, cosine_logit_scale):
    rows, cols, attention_span = padded_part.shape
    focus_groups = cosine_logit_scale.shape[0]
    head_dim = attention_span // focus_groups
    qkv = jnp.dot(padded_part.reshape(-1, attention_span), query_keyvalue_lift, preferred_element_type=jnp.float32).astype(jnp.bfloat16)
    qkv = qkv.reshape(rows // PANE_SIDE, PANE_SIDE, cols // PANE_SIDE, PANE_SIDE, 3 * attention_span)
    qkv = qkv.transpose(0, 2, 1, 3, 4).reshape(-1, PANE_SIDE * PANE_SIDE, 3, focus_groups, head_dim)
    query = unit_rows(qkv[:, :, 0])
    key_rows = unit_rows(qkv[:, :, 1])
    value_rows = qkv[:, :, 2]
    affinity_logits = jnp.einsum('bihd,bjhd->bhij', query.astype(jnp.float32), key_rows.astype(jnp.float32))
    affinity_logits = affinity_logits * cosine_logit_scale[None, :, None, None]
    weights = jnp.exp(affinity_logits)
    probs = (weights / lax.optimization_barrier(jnp.sum(weights, axis=-1, keepdims=True))).astype(jnp.bfloat16)
    mixed_outcome = jnp.einsum('bhij,bjhd->bihd', probs.astype(jnp.float32), value_rows.astype(jnp.float32))
    mixed_outcome = mixed_outcome.astype(jnp.bfloat16).reshape(rows // PANE_SIDE, cols // PANE_SIDE, PANE_SIDE, PANE_SIDE, attention_span)
    return mixed_outcome.transpose(0, 2, 1, 3, 4).reshape(rows, cols, attention_span)

def hidden_ensemble_draw(ensemble_draw_vector_state, patch_lifting, query_keyvalue_lift, output_combiner, cosine_logit_scale):
    rows, cols, feats = ensemble_draw_vector_state.shape
    attention_span = patch_lifting.shape[1]
    hidden = jnp.dot(ensemble_draw_vector_state.reshape(-1, feats), patch_lifting, preferred_element_type=jnp.float32)
    hidden = hidden.astype(jnp.bfloat16).reshape(rows, cols, attention_span)
    normed = layer_norm(hidden).astype(jnp.bfloat16)
    rolled_sequence = jnp.roll(normed, -(PANE_SIDE // 2), axis=1)
    mixed_outcome = jnp.roll(pane_cosine_mixer(rolled_sequence, query_keyvalue_lift, cosine_logit_scale), PANE_SIDE // 2, axis=1)
    mixed = hidden.astype(jnp.float32) + jnp.dot(mixed_outcome.reshape(-1, attention_span), output_combiner, preferred_element_type=jnp.float32).reshape(rows, cols, attention_span)
    return layer_norm(mixed).astype(jnp.bfloat16)

def batched(left, right):
    return jnp.einsum('rij,rjk->rik', left, right, precision=lax.Precision.HIGHEST)

def local_analysis(embedded_patches, decoder_linear_map, sensor_gridpoint, sensor_domain_index, sensor_channel_list, sensor_reading, sensor_noise_deviation, sensor_variable_loadings):
    members, regions, attention_span = embedded_patches.shape
    feats = decoder_linear_map.shape[1]
    channels, variables = sensor_variable_loadings.shape
    points = feats // variables
    count = sensor_gridpoint.shape[0]
    prior_member_grids = jnp.dot(embedded_patches.reshape(-1, attention_span), decoder_linear_map, preferred_element_type=jnp.float32).astype(jnp.bfloat16)
    token = sensor_gridpoint // points
    point = sensor_gridpoint - token * points
    pick_point = (point[:, None] == jnp.arange(points, dtype=jnp.int32)[None, :]).astype(jnp.float32)
    pick_chan = (sensor_channel_list[:, None] == jnp.arange(channels, dtype=jnp.int32)[None, :]).astype(jnp.float32)
    rows_h = jnp.dot(pick_chan, sensor_variable_loadings.astype(jnp.float32), precision=lax.Precision.HIGHEST)
    measurement_mapping = (pick_point[:, :, None] * rows_h[:, None, :]).reshape(count, feats).astype(jnp.bfloat16)
    mapped_samples = jnp.einsum('df,lf->dl', prior_member_grids.astype(jnp.float32), measurement_mapping.astype(jnp.float32))
    mapped_samples = mapped_samples.reshape(members, regions, count)
    pick_token = (token[None, :] == jnp.arange(regions, dtype=jnp.int32)[:, None]).astype(jnp.float32)
    ens_obs = lax.optimization_barrier(jnp.sum(mapped_samples * pick_token[None], axis=1))
    mean_obs = lax.optimization_barrier(jnp.mean(ens_obs, axis=0))
    pert_obs = ens_obs - mean_obs[None, :]
    innovation = sensor_reading - mean_obs
    distance = (token - sensor_domain_index).astype(jnp.float32)
    obs_weight = jnp.exp(-0.5 * distance * distance) / (sensor_noise_deviation * sensor_noise_deviation)
    pick_region = (sensor_domain_index[:, None] == jnp.arange(regions, dtype=jnp.int32)[None, :]).astype(jnp.float32)
    weighted = pert_obs * obs_weight[None, :]
    gram = jnp.einsum('kj,jr,lj->rkl', weighted, pick_region, pert_obs, precision=lax.Precision.HIGHEST)
    drive = jnp.einsum('kj,jr,j->rk', weighted, pick_region, innovation, precision=lax.Precision.HIGHEST)
    eye = jnp.eye(members, dtype=jnp.float32)
    system = eye[None] + gram / (members - 1.0)
    bound = lax.optimization_barrier(jnp.max(lax.optimization_barrier(jnp.sum(jnp.abs(system), axis=2)), axis=1))
    iterate = system / bound[:, None, None]
    inverse_root = jnp.broadcast_to(eye, system.shape)
    for step in range(NS_ITERS):
        factor = 1.5 * eye[None] - 0.5 * batched(inverse_root, iterate)
        iterate = batched(iterate, factor)
        inverse_root = batched(factor, inverse_root)
    root = inverse_root * lax.rsqrt(bound)[:, None, None]
    inner = jnp.einsum('rkl,rl->rk', root, drive, precision=lax.Precision.HIGHEST)
    mean_weight = jnp.einsum('rkl,rl->rk', root, inner, precision=lax.Precision.HIGHEST) / (members - 1.0)
    transform_matrix = root + mean_weight[:, :, None]
    values = embedded_patches.astype(jnp.float32)
    center = lax.optimization_barrier(jnp.mean(values, axis=0))
    spread = values - center[None]
    posterior = center[None] + jnp.einsum('ktf,tkm->mtf', spread, transform_matrix, precision=lax.Precision.HIGHEST)
    posterior = posterior.astype(jnp.bfloat16)
    analysed = jnp.dot(posterior.reshape(-1, attention_span), decoder_linear_map, preferred_element_type=jnp.float32)
    return analysed.astype(jnp.bfloat16).reshape(members, regions, feats)

def reference(starting_ensemble, patch_lifting, query_keyvalue_lift, output_combiner, decoder_linear_map, cosine_logit_scale, sensor_variable_loadings, sensor_gridpoint, sensor_domain_index, sensor_channel_list, sensor_reading, sensor_noise_deviation):
    embedded_patches = lax.map(lambda single_pane: hidden_ensemble_draw(single_pane, patch_lifting, query_keyvalue_lift, output_combiner, cosine_logit_scale), starting_ensemble)
    pieces = embedded_patches.reshape(ENS, LAT, N_TILE, LON_DEV, D).transpose(2, 0, 1, 3, 4)
    pieces = pieces.reshape(N_TILE, ENS, N_MEM, TOKP, D).transpose(2, 0, 1, 3, 4)
    pieces = pieces.reshape(N_MEM * N_TILE, ENS, TOKP, D)
    flat = N_MEM * N_TILE

    def one_piece(items):
        return local_analysis(items[0], decoder_linear_map, items[1], items[2], items[3], items[4], items[5], sensor_variable_loadings)
    analysed = lax.map(one_piece, (pieces, sensor_gridpoint.reshape(flat, OBS_DEV), sensor_domain_index.reshape(flat, OBS_DEV), sensor_channel_list.reshape(flat, OBS_DEV), sensor_reading.reshape(flat, OBS_DEV), sensor_noise_deviation.reshape(flat, OBS_DEV)))
    analysed = analysed.reshape(N_MEM, N_TILE, ENS, TOKP, FEAT).transpose(2, 1, 0, 3, 4)
    analysed = analysed.reshape(ENS, N_TILE, LAT, LON_DEV, FEAT).transpose(0, 2, 1, 3, 4)
    return analysed.reshape(ENS, LAT, LON, FEAT)
```

```python
import numpy as np
import jax
import jax.numpy as jnp
from jax import lax
from jax.sharding import Mesh, PartitionSpec as P

PANE_SIDE = 8
HALF = PANE_SIDE // 2
NS_ITERS = 5
PLANE = ("x", "y")
MEM = ("x", "y", "zh")
TILE = ("zl", "core")
BLOCK = 40

eps_norm = 1e-05
normalizing_guard = 1e-06
bf16 = jnp.bfloat16
f32 = jnp.float32


def swapped(value, axis):
    return lax.ppermute(value, axis, [(0, 1), (1, 0)])


def passed_along(value, axis, by):
    devices = lax.axis_size(axis)
    return lax.ppermute(value, axis, [(i, (i + by) % devices) for i in range(devices)])


def gathered_plane(part):
    copies = lax.optimization_barrier(jnp.broadcast_to(part[None], (16,) + part.shape))
    return lax.all_to_all(copies, PLANE, split_axis=0, concat_axis=0, tiled=True)


def layer_norm(values):
    values = values.astype(f32)
    center = values - jnp.mean(values, axis=-1, keepdims=True)
    spread = jnp.mean(center * center, axis=-1, keepdims=True)
    return center * lax.rsqrt(spread + eps_norm)


def unit_rows(values):
    values = values.astype(f32)
    return (
        values * lax.rsqrt(jnp.sum(values * values, axis=-1, keepdims=True) + normalizing_guard)
    ).astype(bf16)


def times(left, right):
    return jnp.dot(left, right, preferred_element_type=f32)


def times_t(left, right):
    return lax.dot_general(left, right, (((1,), (1,)), ((), ())), preferred_element_type=f32)


def in_order(flag, first, second, axis):
    low = jnp.where(flag == 0, first, second)
    high = jnp.where(flag == 0, second, first)
    return jnp.concatenate([low, high], axis=axis)


def halves(flag, value):
    width = value.shape[-1] // 2
    low, high = value[..., :width], value[..., width:]
    return jnp.where(flag == 0, low, high), jnp.where(flag == 0, high, low)


def batched(left, right):
    return jnp.einsum("rij,rjk->rik", left, right, precision=lax.Precision.HIGHEST)


def attention(qkv, scale):
    panes = qkv.shape[0]
    heads = scale.shape[0]
    own = PANE_SIDE * HALF
    width = qkv.shape[-1] // 3
    split = qkv.reshape(panes, PANE_SIDE * PANE_SIDE, 3, heads, width // heads)
    query = unit_rows(split[:, :own, 0])
    key_rows = unit_rows(split[:, :, 1])
    value_rows = split[:, :, 2]
    scores = jnp.einsum("bihd,bjhd->bhij", query, key_rows, preferred_element_type=f32)
    weights = jnp.exp(scores * scale[None, :, None, None])
    probs = (weights / jnp.sum(weights, axis=-1, keepdims=True)).astype(bf16)
    context = jnp.einsum("bhij,bjhd->bihd", probs, value_rows, preferred_element_type=f32)
    return context.astype(bf16).reshape(panes * own, width)


def obs_setup(obs, loadings):
    points = 16
    grid = obs[:, 0].astype(jnp.int32)
    block = jnp.arange(2, dtype=jnp.int32)[:, None] * 2
    token = grid // points
    point = (grid - token * points).reshape(-1)
    domain = obs[:, 1].astype(jnp.int32)
    channel = obs[:, 2].astype(jnp.int32).reshape(-1)
    distance = (token - domain).astype(f32)
    noise = obs[:, 4]
    weight = (jnp.exp(-0.5 * distance * distance) / (noise * noise)).reshape(-1)
    token = (token + block).reshape(-1)
    domain = (domain + block).reshape(-1)
    pick_point = (point[:, None] == jnp.arange(points, dtype=jnp.int32)[None, :]).astype(bf16)
    pick_chan = (channel[:, None] == jnp.arange(16, dtype=jnp.int32)[None, :]).astype(bf16)
    rows_h = times(pick_chan, loadings).astype(bf16)
    mapping = (pick_point[:, :, None] * rows_h[:, None, :]).reshape(point.shape[0], -1)
    pick_token = (token[None, :] == jnp.arange(4, dtype=jnp.int32)[:, None]).astype(f32)
    pick_region = (domain[None, :] == jnp.arange(4, dtype=jnp.int32)[:, None]).astype(f32)
    return mapping, pick_token, pick_region * weight[None, :], obs[:, 3].reshape(-1)


def transforms(ens_obs, region_weight, reading, own_members):
    members = ens_obs.shape[0]
    mean_obs = jnp.mean(ens_obs, axis=0)
    pert = ens_obs - mean_obs[None, :]
    innovation = reading - mean_obs
    weighted = pert[None] * region_weight[:, None, :]
    gram = jnp.einsum("rkj,lj->rkl", weighted, pert, precision=lax.Precision.HIGHEST)
    drive = jnp.einsum("rkj,j->rk", weighted, innovation, precision=lax.Precision.HIGHEST)
    eye = jnp.eye(members, dtype=f32)
    system = eye[None] + gram / (members - 1.0)
    bound = jnp.max(jnp.sum(jnp.abs(system), axis=2), axis=1)
    iterate = system / bound[:, None, None]
    inverse_root = jnp.broadcast_to(eye, system.shape)
    for step in range(NS_ITERS):
        factor = 1.5 * eye[None] - 0.5 * batched(inverse_root, iterate)
        iterate = batched(iterate, factor)
        inverse_root = batched(factor, inverse_root)
    root = inverse_root * lax.rsqrt(bound)[:, None, None]
    inner = jnp.einsum("rkl,rl->rk", root, drive, precision=lax.Precision.HIGHEST)
    mean_weight = jnp.einsum("rkl,rl->rk", root, inner, precision=lax.Precision.HIGHEST) / (
        members - 1.0
    )
    return root[:, :, :own_members] + mean_weight[:, :, None]


def per_device(
    starting_ensemble,
    patch_lifting,
    query_keyvalue_lift,
    output_combiner,
    decoder_linear_map,
    cosine_logit_scale,
    sensor_variable_loadings,
    sensor_gridpoint,
    sensor_domain_index,
    sensor_channel_list,
    sensor_reading,
    sensor_noise_deviation,
):
    members, rows, cols, feats = starting_ensemble.shape
    width = patch_lifting.shape[1]
    core = lax.axis_index("core")
    zh = lax.axis_index("zh")
    shard = patch_lifting.shape[0]

    fill = ((0, BLOCK - shard), (0, 0))
    packed = jnp.concatenate(
        [
            jnp.pad(patch_lifting, fill),
            query_keyvalue_lift.T,
            output_combiner.T,
            jnp.pad(decoder_linear_map.T, fill),
        ],
        axis=0,
    )
    mine, _ = halves(core, packed)
    front = BLOCK + query_keyvalue_lift.shape[1] + output_combiner.shape[1]
    theirs = swapped(mine, "zh")
    own_front = gathered_plane(mine[:front])
    theirs, own_front = lax.optimization_barrier((theirs, own_front))
    other_front = gathered_plane(theirs[:front])
    tail_rows = in_order(zh, mine[front:], theirs[front:], 0)
    tail_rows, other_front = lax.optimization_barrier((tail_rows, other_front))
    tail_mine = gathered_plane(tail_rows)
    own_front_p = swapped(own_front, "core")
    other_front_p = swapped(other_front, "core")
    tail_part = swapped(tail_mine, "core")

    obs = jnp.stack(
        [
            sensor_gridpoint.reshape(-1).astype(f32),
            sensor_domain_index.reshape(-1).astype(f32),
            sensor_channel_list.reshape(-1).astype(f32),
            sensor_reading.reshape(-1),
            sensor_noise_deviation.reshape(-1),
        ]
    )
    obs = in_order(zh, obs[None], swapped(obs, "zh")[None], 0)
    mapping, pick_token, region_weight, reading = obs_setup(obs, sensor_variable_loadings)

    own_x = starting_ensemble.reshape(members, rows, 2, HALF, feats).transpose(0, 2, 1, 3, 4)
    own_x = own_x.reshape(members, 2, rows * HALF, feats)
    both = jnp.concatenate([own_x, swapped(own_x, "zh")], axis=0)
    west = passed_along(both[:, 1], TILE, 1)
    east = passed_along(both[:, 0], TILE, -1)
    halo = jnp.stack([west, east], axis=1)
    panes = jnp.concatenate([both, halo], axis=2)
    count = 4 * members * rows * cols
    states = panes.reshape(count, feats)

    place = jnp.arange(2 * 16 * BLOCK, dtype=jnp.int32)
    side, rest = place // (16 * BLOCK), place % (16 * BLOCK)
    plane, inside = rest // BLOCK, rest % BLOCK
    source = (plane * 2 + jnp.where(side == 0, zh, 1 - zh)) * shard + inside
    source = jnp.where(inside < shard, source, -1)
    pick = (jnp.arange(feats, dtype=jnp.int32)[:, None] == source[None, :]).astype(bf16)
    spread_states = times(states, pick).astype(bf16)
    xa, xb = spread_states[:, : 16 * BLOCK], spread_states[:, 16 * BLOCK :]

    def embed(own, other):
        return times(xa, own[:, :BLOCK].reshape(-1, own.shape[-1])) + times(
            xb, other[:, :BLOCK].reshape(-1, own.shape[-1])
        )

    hidden = in_order(
        core, embed(own_front, other_front), embed(own_front_p, other_front_p), 1
    ).astype(bf16)
    normed = layer_norm(hidden).astype(bf16)

    def lay(own, other, start, stop):
        own, other = own[:, None, start:stop], other[:, None, start:stop]
        return in_order(zh, own, other, 1).reshape(-1, own.shape[-1])

    q_end = BLOCK + query_keyvalue_lift.shape[1]
    n_mine, n_part = halves(core, normed)
    qkv = (
        times_t(n_mine, lay(own_front, other_front, BLOCK, q_end))
        + times_t(n_part, lay(own_front_p, other_front_p, BLOCK, q_end))
    ).astype(bf16)
    context = attention(
        qkv.reshape(4 * members, PANE_SIDE * PANE_SIDE, qkv.shape[-1]), cosine_logit_scale
    )
    c_mine, c_part = halves(core, context)
    mixed = (
        times_t(c_mine, lay(own_front, other_front, q_end, front))
        + times_t(c_part, lay(own_front_p, other_front_p, q_end, front))
    )
    own_hidden = hidden.reshape(4 * members, 2, rows * HALF, width)[:, 0].reshape(-1, width)
    latent = layer_norm(own_hidden.astype(f32) + mixed).astype(bf16)

    latent = latent.reshape(2 * members, 2, rows, HALF, width).transpose(2, 1, 0, 3, 4)
    moved = lax.all_to_all(
        latent.reshape(16, 2 * members, HALF, width), PLANE, split_axis=0, concat_axis=0, tiled=True
    )
    ensemble = jnp.concatenate(
        [
            moved[:, :members].reshape(16 * members, HALF, width),
            moved[:, members:].reshape(16 * members, HALF, width),
        ],
        axis=0,
    )
    own_members = 16 * members

    def strip(tail):
        return tail.reshape(32, BLOCK, -1)[:, :shard].reshape(feats, -1)

    dec_mine, dec_part = strip(tail_mine), strip(tail_part)

    def decode(values):
        v_mine, v_part = halves(core, values)
        return (times_t(v_mine, dec_mine) + times_t(v_part, dec_part)).astype(bf16)

    forecast = decode(ensemble.reshape(-1, width))
    mapped = times_t(forecast, mapping).reshape(2 * own_members, HALF, -1)
    ens_obs = jnp.sum(mapped * pick_token[None], axis=1)
    transform = transforms(ens_obs, region_weight, reading, own_members)
    values = ensemble.astype(f32)
    center = jnp.mean(values, axis=0)
    posterior = center[None] + jnp.einsum(
        "ktf,tkm->mtf", values - center[None], transform, precision=lax.Precision.HIGHEST
    )
    posterior = posterior.astype(bf16).reshape(16, members, HALF, width)
    back = lax.all_to_all(posterior, PLANE, split_axis=0, concat_axis=0, tiled=True)
    back = back.reshape(rows, 2, members, HALF, width).transpose(2, 0, 1, 3, 4)
    return decode(back.reshape(-1, width)).reshape(members, rows, cols, feats)


def solution(mesh):
    fine = Mesh(
        np.asarray(mesh.devices).reshape(4, 4, 2, 8, 2), ("x", "y", "zh", "zl", "core")
    )
    return jax.shard_map(
        per_device,
        mesh=fine,
        in_specs=(
            P(MEM, None, TILE, None),
            P(MEM, None),
            P(None, MEM),
            P(None, MEM),
            P(None, MEM),
            P(),
            P(),
            P(MEM, TILE, None),
            P(MEM, TILE, None),
            P(MEM, TILE, None),
            P(MEM, TILE, None),
            P(MEM, TILE, None),
        ),
        out_specs=P(MEM, None, TILE, None),
        check_vma=False,
    )
```

```python
import functools

import numpy as np
import jax
import jax.numpy as jnp
from jax import lax
from jax.experimental import pallas as pl
from jax.experimental.pallas import tpu as pltpu
from jax.sharding import Mesh, PartitionSpec as P

PANE_SIDE = 8
HALF = PANE_SIDE // 2
NS_ITERS = 5
PLANE = ("x", "y")
MEM = ("x", "y", "zh")
TILE = ("zl", "core")
BLOCK = 40
SHARD = 35
SIDE = 16 * BLOCK
HEAD = 64
GROUP = 4 * HEAD
OWN = PANE_SIDE * HALF

eps_norm = 1e-05
normalizing_guard = 1e-06
bf16 = jnp.bfloat16
f32 = jnp.float32


def swapped(value, axis):
    return lax.ppermute(value, axis, [(0, 1), (1, 0)])


def passed_along(value, axis, by):
    devices = lax.axis_size(axis)
    return lax.ppermute(value, axis, [(i, (i + by) % devices) for i in range(devices)])


def copies_of(part):
    return lax.optimization_barrier(jnp.broadcast_to(part[None], (16,) + part.shape))


def exchanged(blocks):
    return lax.all_to_all(blocks, PLANE, split_axis=0, concat_axis=0, tiled=True)


def times(left, right):
    return jnp.dot(left, right, preferred_element_type=f32)


def times_t(left, right):
    return lax.dot_general(left, right, (((1,), (1,)), ((), ())), preferred_element_type=f32)


def normalized(values):
    center = values - jnp.mean(values, axis=-1, keepdims=True)
    spread = jnp.mean(center * center, axis=-1, keepdims=True)
    return center * lax.rsqrt(spread + eps_norm)


def in_order(flag, first, second, axis):
    low = jnp.where(flag == 0, first, second)
    high = jnp.where(flag == 0, second, first)
    return jnp.concatenate([low, high], axis=axis)


def halves(flag, value):
    width = value.shape[-1] // 2
    low, high = value[..., :width], value[..., width:]
    return jnp.where(flag == 0, low, high), jnp.where(flag == 0, high, low)


def two_parts(value):
    high = value.astype(bf16)
    return high, (value - high.astype(f32)).astype(bf16)


def three_parts(value):
    high = value.astype(bf16)
    rest = value - high.astype(f32)
    middle = rest.astype(bf16)
    return high, middle, (rest - middle.astype(f32)).astype(bf16)


def iota(shape, axis):
    return lax.broadcasted_iota(jnp.int32, shape, axis)


def one_hot(order, width):
    return jnp.asarray(np.asarray(order)[:, None] == np.arange(width)[None, :], bf16)


def attention_kernel(
    flags, own_x, west_x, east_x, e_mine, e_part, w_mine, w_part, scale, hidden_out, context_out
):
    core, zh = flags[0], flags[1]
    members = own_x.shape[2] // OWN
    x = jnp.concatenate(
        [own_x[0, 0], own_x[0, 1], west_x[0], east_x[0]], axis=0
    )
    x_own, x_other = halves(zh, x)
    x = jnp.concatenate([x_own, x_other], axis=1)
    hidden = in_order(core, times(x, e_mine[...]), times(x, e_part[...]), 1).astype(bf16)
    normed = normalized(hidden.astype(f32)).astype(bf16)
    n_mine, n_part = halves(core, normed)
    own_rows = 2 * members * OWN
    hidden_out[...] = hidden[:own_rows]
    width = hidden.shape[1]

    same = (iota((GROUP, GROUP), 0) // HEAD) == (iota((GROUP, GROUP), 1) // HEAD)
    ones = same.astype(bf16)
    lane_head = iota((PANE_SIDE * PANE_SIDE, GROUP), 1) // HEAD

    def projected(left, right, start):
        rows = pl.ds(start, GROUP)
        return (times_t(left, w_mine[rows, :]) + times_t(right, w_part[rows, :])).astype(bf16)

    def unit(values):
        values = values.astype(f32)
        high, low = two_parts(values * values)
        total = times(high, ones) + times(low, ones)
        return (values * lax.rsqrt(total + normalizing_guard)).astype(bf16)

    def diagonal(rows):
        zero = jnp.zeros_like(rows)
        return jnp.concatenate(
            [jnp.where(lane_head == h, rows, zero) for h in range(4)], axis=0
        )

    def pane_rows(values, w, m):
        own = values[(w * members + m) * OWN : (w * members + m + 1) * OWN]
        start = own_rows + (w * members + m) * OWN
        return jnp.concatenate([own, values[start : start + OWN]], axis=0)

    for g in range(width // GROUP):
        at = g * GROUP
        query = unit(projected(n_mine[:own_rows], n_part[:own_rows], at))
        key_rows = unit(projected(n_mine, n_part, width + at))
        value_rows = projected(n_mine, n_part, 2 * width + at)
        scores = []
        for w in range(2):
            for m in range(members):
                first = (w * members + m) * OWN
                scores.append(
                    times_t(query[first : first + OWN], diagonal(pane_rows(key_rows, w, m)))
                )
        weights = jnp.exp(jnp.concatenate(scores, axis=0) * scale[:, at : at + GROUP]).astype(bf16)
        total = times(weights, ones)
        mixed = []
        for w in range(2):
            for m in range(members):
                first = (w * members + m) * OWN
                mixed.append(
                    times(weights[first : first + OWN], diagonal(pane_rows(value_rows, w, m)))
                )
        context_out[:, at : at + GROUP] = (jnp.concatenate(mixed, axis=0) / total).astype(bf16)


def attention(flags, own_x, west_x, east_x, e_mine, e_part, w_mine, w_part, scale):
    groups, panes, pane_own, wide = own_x.shape
    rows = panes * pane_own
    width = 2 * e_mine.shape[1]

    def whole(array):
        return pl.BlockSpec(array.shape, lambda i: (0,) * array.ndim)

    return pl.pallas_call(
        attention_kernel,
        grid=(groups,),
        in_specs=[
            pl.BlockSpec(memory_space=pltpu.SMEM),
            pl.BlockSpec((1, panes, pane_own, wide), lambda i: (i, 0, 0, 0)),
            pl.BlockSpec((1,) + west_x.shape[1:], lambda i: (i, 0, 0)),
            pl.BlockSpec((1,) + east_x.shape[1:], lambda i: (i, 0, 0)),
            whole(e_mine),
            whole(e_part),
            whole(w_mine),
            whole(w_part),
            whole(scale),
        ],
        out_specs=[pl.BlockSpec((rows, width), lambda i: (i, 0))] * 2,
        out_shape=[jax.ShapeDtypeStruct((groups * rows, width), bf16)] * 2,
        compiler_params=pltpu.CompilerParams(vmem_limit_bytes=40 * 1024 * 1024),
        name="attention",
    )(flags, own_x, west_x, east_x, e_mine, e_part, w_mine, w_part, scale)


def latent_kernel(flags, context, hidden, order, t_mine, t_part, latent_out):
    c_mine, c_part = halves(flags[0], context[...])
    outs = t_mine.shape[1] - 16

    def combiner(ref):
        return ref[:, :outs, :].reshape(16 * outs, ref.shape[2])

    mixed = times_t(c_mine, combiner(t_mine)) + times_t(c_part, combiner(t_part))
    latent = normalized(hidden[...].astype(f32) + mixed).astype(bf16)
    latent_out[...] = times(order[...], latent).astype(bf16)


def latent_rows(flags, context, hidden, order, t_mine, t_part):
    vmem = pl.BlockSpec(memory_space=pltpu.VMEM)
    return pl.pallas_call(
        latent_kernel,
        in_specs=[pl.BlockSpec(memory_space=pltpu.SMEM)] + [vmem] * 5,
        out_specs=vmem,
        out_shape=jax.ShapeDtypeStruct(context.shape, bf16),
        compiler_params=pltpu.CompilerParams(vmem_limit_bytes=32 * 1024 * 1024),
        name="latent",
    )(flags, context, hidden, order, t_mine, t_part)


def product(left, right):
    l_high, l_low = two_parts(left)
    r_high, r_low = two_parts(right)
    return times(
        jnp.concatenate([l_high, l_high, l_low], axis=1),
        jnp.concatenate([r_high, r_low, r_high], axis=0),
    )


def product_t(left, right):
    l_high, l_low = two_parts(left)
    r_high, r_low = two_parts(right)
    return times_t(
        jnp.concatenate([l_high, l_high, l_low], axis=1),
        jnp.concatenate([r_high, r_low, r_high], axis=1),
    )


def analysis_kernel(flags, moved, order, back_order, obs, t_mine, t_part, posterior_out):
    core, zh = flags[0], flags[1]
    width = moved.shape[1]
    latent = times(order[...], moved[...]).astype(bf16)
    members = latent.shape[0] // HALF
    l_mine, l_part = halves(core, latent)
    outs = t_mine.shape[1] - 16

    def readers(ref):
        return ref[:, outs:, :].reshape(16 * 16, ref.shape[2])

    seen = times_t(l_mine, readers(t_mine)) + times_t(l_part, readers(t_part))
    places = seen.shape[1]
    eye = (iota((members, members), 0) == iota((members, members), 1)).astype(f32)
    systems, drives = [], []
    for block in range(2):
        ens = [seen[(2 * block + t) * members : (2 * block + t + 1) * members] for t in range(2)]
        mean = [jnp.mean(e, axis=0, keepdims=True) for e in ens]
        pert = jnp.concatenate([e - m for e, m in zip(ens, mean)], axis=1)
        mean = jnp.concatenate(mean, axis=1)
        for r in range(2):
            weight = obs[block, r : r + 1, :]
            read = obs[block, 2 + r : 3 + r, :]
            gram = product_t(pert * weight, pert)
            drives.append(jnp.sum(pert * (read - weight * mean), axis=1, keepdims=True))
            systems.append(eye + gram / (members - 1.0))
    bounds = [
        jnp.max(jnp.sum(jnp.abs(s), axis=1, keepdims=True), axis=0, keepdims=True) for s in systems
    ]
    iterates = [s / b for s, b in zip(systems, bounds)]
    factors = [1.5 * eye - 0.5 * y for y in iterates]
    iterates = [product(y, f) for y, f in zip(iterates, factors)]
    roots = factors
    for step in range(1, NS_ITERS):
        factors = [1.5 * eye - 0.5 * product(z, y) for z, y in zip(roots, iterates)]
        if step + 1 < NS_ITERS:
            iterates = [product(y, f) for y, f in zip(iterates, factors)]
        roots = [product(f, z) for f, z in zip(factors, roots)]
    results = []
    for region in range(2 * 2):
        root = roots[region] * lax.rsqrt(bounds[region])
        inner = jnp.sum(root * drives[region], axis=0, keepdims=True)
        mean_weight = jnp.sum(root * inner, axis=1, keepdims=True) / (members - 1.0)
        transform = root + mean_weight
        own = jnp.where(zh == 0, transform[:, : members // 2], transform[:, members // 2 :])
        values = latent[region * members : (region + 1) * members]
        center = jnp.mean(values.astype(f32), axis=0, keepdims=True)
        own_t = own.T
        high, middle, low = three_parts(own_t)
        left = jnp.concatenate([high, middle, low], axis=1)
        moved_part = times(left, jnp.concatenate([values] * 3, axis=0))
        share = 1.0 - jnp.sum(own_t, axis=1, keepdims=True)
        results.append((moved_part + share * center).astype(bf16))
    posterior = jnp.concatenate(results, axis=0)
    posterior_out[...] = times(back_order[...], posterior).astype(bf16)


def analysis(flags, moved, order, back_order, obs, t_mine, t_part):
    vmem = pl.BlockSpec(memory_space=pltpu.VMEM)
    return pl.pallas_call(
        analysis_kernel,
        in_specs=[pl.BlockSpec(memory_space=pltpu.SMEM)] + [vmem] * 6,
        out_specs=vmem,
        out_shape=jax.ShapeDtypeStruct((back_order.shape[0], moved.shape[1]), bf16),
        compiler_params=pltpu.CompilerParams(vmem_limit_bytes=32 * 1024 * 1024),
        name="analysis",
    )(flags, moved, order, back_order, obs, t_mine, t_part)


def packed_obs(grid, domain, channel, reading, noise, width):
    rows = [grid.astype(bf16), domain.astype(bf16), channel.astype(bf16)]
    rows += list(three_parts(reading)) + list(three_parts(noise))
    table = jnp.stack(rows)
    return jnp.pad(table, ((0, 16 - len(rows)), (0, width - table.shape[1])))


def weighted_places(table, count):
    table = table[:, :, :count].astype(f32)
    grid = table[:, 0].astype(jnp.int32)
    domain = table[:, 1].astype(jnp.int32)
    channel = table[:, 2].astype(jnp.int32)
    reading = table[:, 3] + (table[:, 4] + table[:, 5])
    noise = table[:, 6] + (table[:, 7] + table[:, 8])
    token = grid // 16
    distance = (token - domain).astype(f32)
    weight = jnp.exp(-0.5 * distance * distance) / (noise * noise)
    region = (domain[:, None, :] == jnp.arange(2, dtype=jnp.int32)[None, :, None]).astype(f32)
    weight = region * weight[:, None, :]
    left = jnp.concatenate([weight, weight * reading[:, None, :]], axis=1)
    place = grid * 16 + channel
    pick = (place[:, :, None] == jnp.arange(512, dtype=jnp.int32)[None, None, :]).astype(f32)
    return jnp.einsum("bcj,bjp->bcp", left, pick, precision=lax.Precision.HIGHEST)


def per_device(
    starting_ensemble,
    patch_lifting,
    query_keyvalue_lift,
    output_combiner,
    decoder_linear_map,
    cosine_logit_scale,
    sensor_variable_loadings,
    sensor_gridpoint,
    sensor_domain_index,
    sensor_channel_list,
    sensor_reading,
    sensor_noise_deviation,
):
    members, rows, cols, feats = starting_ensemble.shape
    width = patch_lifting.shape[1]
    core = lax.axis_index("core")
    zh = lax.axis_index("zh")
    flags = jnp.stack([core, zh]).astype(jnp.int32)

    fill = ((0, BLOCK - SHARD), (0, 0))
    packed = jnp.concatenate(
        [
            jnp.pad(patch_lifting, fill),
            query_keyvalue_lift.T,
            output_combiner.T,
            jnp.pad(decoder_linear_map.T, fill),
        ],
        axis=0,
    )
    mine, _ = halves(core, packed)
    q_end = BLOCK + query_keyvalue_lift.shape[1]
    o_end = q_end + output_combiner.shape[1]
    theirs = swapped(mine, "zh")
    own_front = exchanged(copies_of(mine[:q_end]))
    other_copies, own_front = lax.optimization_barrier((copies_of(theirs[:q_end]), own_front))
    other_front = exchanged(other_copies)
    combiner = in_order(zh, mine[q_end:o_end], theirs[q_end:o_end], 0)
    decoder = in_order(zh, mine[o_end:], theirs[o_end:], 0)
    loadings = jnp.pad(
        sensor_variable_loadings.reshape(16, 2, SHARD), ((0, 0), (0, 0), (0, BLOCK - SHARD))
    ).reshape(16, 2 * BLOCK)
    readers = times(loadings, decoder).astype(bf16)
    tail_copies, other_front = lax.optimization_barrier(
        (copies_of(jnp.concatenate([combiner, readers], axis=0)), other_front)
    )
    tail_mine = exchanged(tail_copies)
    dec_mine = lax.all_gather(decoder, PLANE, axis=0, tiled=True)
    own_front_p = swapped(own_front, "core")
    other_front_p = swapped(other_front, "core")
    tail_part = swapped(tail_mine, "core")

    token = np.arange(members * rows * cols).reshape(members, rows, 2, HALF)
    source = (np.arange(16)[None, :, None] * 2 + np.arange(2)[:, None, None]) * SHARD + np.arange(
        BLOCK
    )[None, None, :]
    source = np.where(np.arange(BLOCK)[None, None, :] < SHARD, source, -1).reshape(-1)
    pick_rows = one_hot(token.transpose(2, 0, 1, 3).reshape(-1), token.size)
    pick_cols = (jnp.arange(feats, dtype=jnp.int32)[:, None] == jnp.asarray(source, jnp.int32)[None, :]).astype(bf16)
    states = times(pick_rows, starting_ensemble.reshape(-1, feats)).astype(bf16)
    states = times(states, pick_cols).astype(bf16)
    table = packed_obs(
        sensor_gridpoint.reshape(-1),
        sensor_domain_index.reshape(-1),
        sensor_channel_list.reshape(-1),
        sensor_reading.reshape(-1),
        sensor_noise_deviation.reshape(-1),
        2 * SIDE,
    )
    count = token.size
    both = lax.all_gather(jnp.concatenate([states, table], axis=0), "zh", axis=0, tiled=False)
    own_x = both[:, :count].reshape(2, 2, count // 2, 2 * SIDE)
    west_x = passed_along(own_x[:, 1], TILE, 1)
    east_x = passed_along(own_x[:, 0], TILE, -1)
    obs = weighted_places(both[:, count:], sensor_gridpoint.size)

    def embed_rows(own, other):
        return jnp.concatenate(
            [own[:, :BLOCK].reshape(SIDE, -1), other[:, :BLOCK].reshape(SIDE, -1)], axis=0
        )

    def lifts(own, other):
        own, other = own[:, None, BLOCK:], other[:, None, BLOCK:]
        return in_order(zh, own, other, 1).reshape(-1, own.shape[-1])

    scale = jnp.repeat(cosine_logit_scale, HEAD)[None, :]
    hidden, context = attention(
        flags,
        own_x,
        west_x,
        east_x,
        embed_rows(own_front, other_front),
        embed_rows(own_front_p, other_front_p),
        lifts(own_front, other_front),
        lifts(own_front_p, other_front_p),
        scale,
    )

    size = 2 * count
    grid = np.arange(size).reshape(2, 2, members, rows, HALF)
    order = one_hot(grid.transpose(3, 1, 0, 2, 4).reshape(-1), size)
    latent = latent_rows(flags, context, hidden, order, tail_mine, tail_part)
    moved = exchanged(latent.reshape(16, size // 16, width)).reshape(size, width)

    grid = np.arange(size).reshape(16, 2, members, HALF)
    order = one_hot(grid.transpose(3, 1, 0, 2).reshape(-1), size)
    grid = np.arange(size // 2).reshape(HALF, 16, members)
    back_order = one_hot(grid.transpose(1, 2, 0).reshape(-1), size // 2)
    posterior = analysis(flags, moved, order, back_order, obs, tail_mine, tail_part)
    back = exchanged(posterior.reshape(16, size // 32, width)).reshape(size // 2, width)

    grid = np.arange(size // 2).reshape(rows, 2, members, HALF)
    order = one_hot(grid.transpose(2, 0, 1, 3).reshape(-1), size // 2)
    back = times(order, back).astype(bf16)

    def strip(tail):
        return tail.reshape(32, BLOCK, -1)[:, :SHARD].reshape(feats, -1)

    dec_part = swapped(dec_mine, "core")
    b_mine, b_part = halves(core, back)
    result = times_t(b_mine, strip(dec_mine)) + times_t(b_part, strip(dec_part))
    return result.astype(bf16).reshape(members, rows, cols, feats)


def solution(mesh):
    fine = Mesh(
        np.asarray(mesh.devices).reshape(4, 4, 2, 8, 2), ("x", "y", "zh", "zl", "core")
    )
    return jax.shard_map(
        per_device,
        mesh=fine,
        in_specs=(
            P(MEM, None, TILE, None),
            P(MEM, None),
            P(None, MEM),
            P(None, MEM),
            P(None, MEM),
            P(),
            P(),
            P(MEM, TILE, None),
            P(MEM, TILE, None),
            P(MEM, TILE, None),
            P(MEM, TILE, None),
            P(MEM, TILE, None),
        ),
        out_specs=P(MEM, None, TILE, None),
        check_vma=False,
    )
```

```python
import functools

import numpy as np
import jax
import jax.numpy as jnp
from jax import lax
from jax.experimental import pallas as pl
from jax.experimental.pallas import tpu as pltpu
from jax.sharding import Mesh, PartitionSpec as P

PANE_SIDE = 8
HALF = PANE_SIDE // 2
NS_ITERS = 5
PLANE = ("x", "y")
MEM = ("x", "y", "zh")
TILE = ("zl", "core")
BLOCK = 40
SHARD = 35
SIDE = 16 * BLOCK
HEAD = 64
GROUP = 4 * HEAD
OWN = PANE_SIDE * HALF

eps_norm = 1e-05
normalizing_guard = 1e-06
bf16 = jnp.bfloat16
f32 = jnp.float32


def swapped(value, axis):
    return lax.ppermute(value, axis, [(0, 1), (1, 0)])


def shifted(value, by):
    return lax.ppermute(value, ("zh", "zl"), [(z, (z + by) % 16) for z in range(16)])


def crossed(value):
    pairs = [(8 * h + z, 8 * (1 - h) + (z + 4) % 8) for h in range(2) for z in range(8)]
    return lax.ppermute(value, ("zh", "zl"), pairs)


def between_chips(value):
    pairs = [(2 * z, 2 * ((z - 1) % 8) + 1) for z in range(8)]
    return lax.ppermute(value, TILE, pairs + [(b, a) for a, b in pairs])


def copies_of(part):
    return lax.optimization_barrier(jnp.broadcast_to(part[None], (16,) + part.shape))


def exchanged(blocks):
    return lax.all_to_all(blocks, PLANE, split_axis=0, concat_axis=0, tiled=True)


def times(left, right):
    return jnp.dot(left, right, preferred_element_type=f32)


def times_t(left, right):
    return lax.dot_general(left, right, (((1,), (1,)), ((), ())), preferred_element_type=f32)


def normalized(values):
    center = values - jnp.mean(values, axis=-1, keepdims=True)
    spread = jnp.mean(center * center, axis=-1, keepdims=True)
    return center * lax.rsqrt(spread + eps_norm)


def in_order(flag, first, second, axis):
    low = jnp.where(flag == 0, first, second)
    high = jnp.where(flag == 0, second, first)
    return jnp.concatenate([low, high], axis=axis)


def halves(flag, value):
    width = value.shape[-1] // 2
    low, high = value[..., :width], value[..., width:]
    return jnp.where(flag == 0, low, high), jnp.where(flag == 0, high, low)


def two_parts(value):
    high = value.astype(bf16)
    return high, (value - high.astype(f32)).astype(bf16)


def three_parts(value):
    high = value.astype(bf16)
    rest = value - high.astype(f32)
    middle = rest.astype(bf16)
    return high, middle, (rest - middle.astype(f32)).astype(bf16)


def iota(shape, axis):
    return lax.broadcasted_iota(jnp.int32, shape, axis)


def one_hot(order, width):
    return jnp.asarray(np.asarray(order)[:, None] == np.arange(width)[None, :], bf16)


def front_kernel(
    flags,
    x_all,
    own_m,
    other_m,
    own_p,
    other_p,
    scale,
    order,
    latent_out,
    w_mine,
    w_part,
    latents,
):
    core, zh = flags[0], flags[1]
    members = x_all.shape[1] // (4 * OWN)
    lanes = own_m.shape[2]
    lifts, outs = 6 * lanes // 32, 2 * lanes // 32
    front = lifts + BLOCK
    width = 2 * lanes

    @pl.when(pl.program_id(0) == 0)
    def _():
        for target, own, other in ((w_mine, own_m, other_m), (w_part, own_p, other_p)):
            for place in range(16):
                target[2 * lifts * place : 2 * lifts * (place + 1), :] = in_order(
                    zh, own[place, :lifts, :], other[place, :lifts, :], 0
                )

    def embed(own, other):
        return times(x_own, own[:, lifts:front, :].reshape(SIDE, lanes)) + times(
            x_other, other[:, lifts:front, :].reshape(SIDE, lanes)
        )

    x = x_all[0]
    x_own, x_other = halves(zh, x)
    hidden = in_order(core, embed(own_m, other_m), embed(own_p, other_p), 1).astype(bf16)
    normed = normalized(hidden.astype(f32)).astype(bf16)
    n_mine, n_part = halves(core, normed)
    own_rows = 2 * members * OWN

    same = (iota((GROUP, GROUP), 0) // HEAD) == (iota((GROUP, GROUP), 1) // HEAD)
    ones = same.astype(bf16)
    lane_head = iota((PANE_SIDE * PANE_SIDE, GROUP), 1) // HEAD

    def projected(left, right, start):
        rows = pl.ds(start, GROUP)
        return (times_t(left, w_mine[rows, :]) + times_t(right, w_part[rows, :])).astype(bf16)

    def unit(values):
        values = values.astype(f32)
        high, low = two_parts(values * values)
        total = times(high, ones) + times(low, ones)
        return (values * lax.rsqrt(total + normalizing_guard)).astype(bf16)

    def diagonal(rows):
        zero = jnp.zeros_like(rows)
        return jnp.concatenate([jnp.where(lane_head == h, rows, zero) for h in range(4)], axis=0)

    def pane_rows(values, w, m):
        own = values[(w * members + m) * OWN : (w * members + m + 1) * OWN]
        start = own_rows + (w * members + m) * OWN
        return jnp.concatenate([own, values[start : start + OWN]], axis=0)

    panes = [(w, m) for w in range(2) for m in range(members)]
    context = []
    for g in range(width // GROUP):
        at = g * GROUP
        query = unit(projected(n_mine[:own_rows], n_part[:own_rows], at))
        key_rows = unit(projected(n_mine, n_part, width + at))
        value_rows = projected(n_mine, n_part, 2 * width + at)
        scores = [
            times_t(query[i * OWN : (i + 1) * OWN], diagonal(pane_rows(key_rows, w, m)))
            for i, (w, m) in enumerate(panes)
        ]
        weights = jnp.exp(jnp.concatenate(scores, axis=0) * scale[:, at : at + GROUP]).astype(bf16)
        total = times(weights, ones)
        mixed = [
            times(weights[i * OWN : (i + 1) * OWN], diagonal(pane_rows(value_rows, w, m)))
            for i, (w, m) in enumerate(panes)
        ]
        context.append((jnp.concatenate(mixed, axis=0) / total).astype(bf16))
    c_mine, c_part = halves(core, jnp.concatenate(context, axis=1))

    def combiner(own, other):
        rows = [
            in_order(
                zh, own[place, front : front + outs, :], other[place, front : front + outs, :], 0
            )
            for place in range(16)
        ]
        return jnp.concatenate(rows, axis=0)

    mixed = times_t(c_mine, combiner(own_m, other_m)) + times_t(c_part, combiner(own_p, other_p))
    latent = normalized(hidden[:own_rows].astype(f32) + mixed).astype(bf16)
    latents[pl.ds(pl.multiple_of(pl.program_id(0) * own_rows, own_rows), own_rows), :] = latent

    @pl.when(pl.program_id(0) == pl.num_programs(0) - 1)
    def _():
        latent_out[...] = times(order[...], latents[...]).astype(bf16)


def front_latents(flags, states, weights, scale, order):
    lanes = weights[0].shape[2]
    groups, count, wide = states.shape
    shape = (order.shape[0], 2 * lanes)

    def whole(array):
        return pl.BlockSpec(
            array.shape, lambda i: (0,) * array.ndim, pipeline_mode=pl.Buffered(1)
        )

    return pl.pallas_call(
        front_kernel,
        grid=(groups,),
        in_specs=[
            pl.BlockSpec(memory_space=pltpu.SMEM),
            pl.BlockSpec((1, count, wide), lambda i: (i, 0, 0)),
        ]
        + [whole(v) for v in (*weights, scale, order)],
        out_specs=pl.BlockSpec(shape, lambda i: (0, 0)),
        out_shape=jax.ShapeDtypeStruct(shape, bf16),
        scratch_shapes=[pltpu.VMEM((6 * lanes, lanes), bf16)] * 2 + [pltpu.VMEM(shape, bf16)],
        compiler_params=pltpu.CompilerParams(vmem_limit_bytes=32 * 1024 * 1024),
        name="front",
    )(flags, states, *weights, scale, order)


def prepare_kernel(x, order, grid, domain, channel, reading, noise, packed):
    count = x.shape[0]
    packed[:count, :] = times(order[...], x[...]).astype(bf16)
    table = [grid[...].astype(f32), domain[...].astype(f32), channel[...].astype(f32)]
    table = [t.astype(bf16) for t in table]
    table += list(three_parts(reading[...])) + list(three_parts(noise[...]))
    table = jnp.concatenate([t.astype(f32) for t in table], axis=0)
    packed[count:, :] = jnp.zeros((16, packed.shape[1]), bf16)
    table = jnp.concatenate([table, jnp.zeros((16 - table.shape[0], table.shape[1]), f32)], axis=0)
    packed[count:, : table.shape[1]] = table.astype(bf16)


def prepare(x, order, *obs):
    vmem = pl.BlockSpec(memory_space=pltpu.VMEM)
    count, feats = x.shape
    return pl.pallas_call(
        prepare_kernel,
        in_specs=[vmem] * (2 + len(obs)),
        out_specs=vmem,
        out_shape=jax.ShapeDtypeStruct((count + 16, feats), bf16),
        name="prepare",
    )(x, order, *obs)


def product(left, right):
    l_high, l_low = two_parts(left)
    r_high, r_low = two_parts(right)
    return times(
        jnp.concatenate([l_high, l_high, l_low], axis=1),
        jnp.concatenate([r_high, r_low, r_high], axis=0),
    )


def product_t(left, right):
    l_high, l_low = two_parts(left)
    r_high, r_low = two_parts(right)
    return times_t(
        jnp.concatenate([l_high, l_high, l_low], axis=1),
        jnp.concatenate([r_high, r_low, r_high], axis=1),
    )


def analysis_kernel(flags, moved, order, back_order, obs, t_mine, t_part, posterior_out):
    latent = times(order[...], moved[...]).astype(bf16)
    members = latent.shape[0] // HALF
    l_mine, l_part = halves(flags[0], latent)

    def readers(ref):
        return ref[:, ref.shape[1] - 16 :, :].reshape(16 * 16, ref.shape[2])

    seen = times_t(l_mine, readers(t_mine)) + times_t(l_part, readers(t_part))
    eye = (iota((members, members), 0) == iota((members, members), 1)).astype(f32)
    systems, drives = [], []
    for block in range(2):
        ens = [seen[(2 * block + t) * members : (2 * block + t + 1) * members] for t in range(2)]
        mean = [jnp.mean(e, axis=0, keepdims=True) for e in ens]
        pert = jnp.concatenate([e - m for e, m in zip(ens, mean)], axis=1)
        mean = jnp.concatenate(mean, axis=1)
        for r in range(2):
            weight = obs[block, r : r + 1, :]
            read = obs[block, 2 + r : 3 + r, :]
            gram = product_t(pert * weight, pert)
            drives.append(jnp.sum(pert * (read - weight * mean), axis=1, keepdims=True))
            systems.append(eye + gram / (members - 1.0))
    bounds = [
        jnp.max(jnp.sum(jnp.abs(s), axis=1, keepdims=True), axis=0, keepdims=True) for s in systems
    ]
    iterates = [s / b for s, b in zip(systems, bounds)]
    factors = [1.5 * eye - 0.5 * y for y in iterates]
    iterates = [product(y, f) for y, f in zip(iterates, factors)]
    roots = factors
    for step in range(1, NS_ITERS):
        factors = [1.5 * eye - 0.5 * product(z, y) for z, y in zip(roots, iterates)]
        if step + 1 < NS_ITERS:
            iterates = [product(y, f) for y, f in zip(iterates, factors)]
        roots = [product(f, z) for f, z in zip(factors, roots)]
    results = []
    for region in range(2 * 2):
        root = roots[region] * lax.rsqrt(bounds[region])
        inner = jnp.sum(root * drives[region], axis=0, keepdims=True)
        mean_weight = jnp.sum(root * inner, axis=1, keepdims=True) / (members - 1.0)
        transform = root + mean_weight
        own_t = transform[:, : members // 2].T
        values = latent[region * members : (region + 1) * members]
        center = jnp.mean(values.astype(f32), axis=0, keepdims=True)
        high, middle, low = three_parts(own_t)
        left = jnp.concatenate([high, middle, low], axis=1)
        moved_part = times(left, jnp.concatenate([values] * 3, axis=0))
        share = 1.0 - jnp.sum(own_t, axis=1, keepdims=True)
        results.append((moved_part + share * center).astype(bf16))
    posterior = jnp.concatenate(results, axis=0)
    posterior_out[...] = times(back_order[...], posterior).astype(bf16)


def analysis(flags, moved, order, back_order, obs, t_mine, t_part):
    vmem = pl.BlockSpec(memory_space=pltpu.VMEM)
    return pl.pallas_call(
        analysis_kernel,
        in_specs=[pl.BlockSpec(memory_space=pltpu.SMEM)] + [vmem] * 6,
        out_specs=vmem,
        out_shape=jax.ShapeDtypeStruct((back_order.shape[0], moved.shape[1]), bf16),
        compiler_params=pltpu.CompilerParams(vmem_limit_bytes=32 * 1024 * 1024),
        name="analysis",
    )(flags, moved, order, back_order, obs, t_mine, t_part)


def decode_kernel(flags, parts, order, d_mine, d_part, out):
    b_mine, b_part = halves(flags[0], times(order[...], parts[...]).astype(bf16))
    out[...] = (times_t(b_mine, d_mine[...]) + times_t(b_part, d_part[...])).astype(bf16)


def decode(flags, parts, order, d_mine, d_part):
    vmem = pl.BlockSpec(memory_space=pltpu.VMEM)
    return pl.pallas_call(
        decode_kernel,
        in_specs=[pl.BlockSpec(memory_space=pltpu.SMEM)] + [vmem] * 4,
        out_specs=vmem,
        out_shape=jax.ShapeDtypeStruct((order.shape[0], d_mine.shape[0]), bf16),
        compiler_params=pltpu.CompilerParams(vmem_limit_bytes=32 * 1024 * 1024),
        name="decode",
    )(flags, parts, order, d_mine, d_part)


def weighted_places(table, count):
    table = table[:, :, :count].astype(f32)
    grid = table[:, 0].astype(jnp.int32)
    domain = table[:, 1].astype(jnp.int32)
    channel = table[:, 2].astype(jnp.int32)
    reading = table[:, 3] + (table[:, 4] + table[:, 5])
    noise = table[:, 6] + (table[:, 7] + table[:, 8])
    token = grid // 16
    distance = (token - domain).astype(f32)
    weight = jnp.exp(-0.5 * distance * distance) / (noise * noise)
    region = (domain[:, None, :] == jnp.arange(2, dtype=jnp.int32)[None, :, None]).astype(f32)
    weight = region * weight[:, None, :]
    left = jnp.concatenate([weight, weight * reading[:, None, :]], axis=1)
    place = grid * 16 + channel
    pick = (place[:, :, None] == jnp.arange(512, dtype=jnp.int32)[None, None, :]).astype(f32)
    return jnp.einsum("bcj,bjp->bcp", left, pick, precision=lax.Precision.HIGHEST)


def per_device(
    starting_ensemble,
    patch_lifting,
    query_keyvalue_lift,
    output_combiner,
    decoder_linear_map,
    cosine_logit_scale,
    sensor_variable_loadings,
    sensor_gridpoint,
    sensor_domain_index,
    sensor_channel_list,
    sensor_reading,
    sensor_noise_deviation,
):
    members, rows, cols, feats = starting_ensemble.shape
    width = patch_lifting.shape[1]
    core = lax.axis_index("core")
    zh = lax.axis_index("zh")
    flags = jnp.stack([core, zh]).astype(jnp.int32)

    fill = ((0, BLOCK - SHARD), (0, 0))
    packed = jnp.concatenate(
        [
            query_keyvalue_lift.T,
            jnp.pad(patch_lifting, fill),
            output_combiner.T,
            jnp.pad(decoder_linear_map.T, fill),
        ],
        axis=0,
    )
    mine, _ = halves(core, packed)
    lanes = mine.shape[1]
    front = query_keyvalue_lift.shape[1] + BLOCK
    o_end = front + output_combiner.shape[1]
    own_all = exchanged(copies_of(mine))

    count = members * rows * cols
    grid = np.arange(count).reshape(members, rows, 2, HALF)
    pick_rows = one_hot(grid.transpose(2, 0, 1, 3).reshape(-1), count)
    obs = (
        sensor_gridpoint,
        sensor_domain_index,
        sensor_channel_list,
        sensor_reading,
        sensor_noise_deviation,
    )
    sent = prepare(
        starting_ensemble.reshape(count, feats), pick_rows, *(o.reshape(1, -1) for o in obs)
    )
    sent, outgoing = lax.optimization_barrier((sent, mine))
    theirs = crossed(outgoing)
    middle = (count + 16) // 2
    up, down = shifted(sent[:middle], 4), shifted(sent[middle:], -4)

    decoder = in_order(zh, mine[o_end:], theirs[o_end:], 0)
    loadings = jnp.pad(
        sensor_variable_loadings.reshape(16, 2, SHARD), ((0, 0), (0, 0), (0, BLOCK - SHARD))
    ).reshape(16, 2 * BLOCK)
    readers = times(loadings, decoder).astype(bf16)
    copies, own_all, up, down = lax.optimization_barrier(
        (copies_of(jnp.concatenate([theirs, readers], axis=0)), own_all, up, down)
    )
    partner = jnp.concatenate([shifted(up, 4), shifted(down, -4)], axis=0)
    other_main = exchanged(copies)
    inside = np.arange(BLOCK)[None, None, :]
    place = np.arange(16)[None, :, None] * 2 + np.arange(2)[:, None, None]
    source = np.where(inside < SHARD, place * SHARD + inside, -1).reshape(-1)
    pick_cols = jnp.asarray(np.arange(feats)[:, None] == source[None, :], bf16)

    both = jnp.stack([sent, partner])
    low, high = both[:, : count // 2], both[:, count // 2 : count]
    core_x = swapped(jnp.where(core == 0, high, low), "core")
    chip_x = between_chips(jnp.where(core == 0, low, high))

    states = jnp.concatenate([both[:, :count], in_order(core, chip_x, core_x, 1)], axis=1)
    states = times(states.reshape(4 * count, feats), pick_cols).astype(bf16)
    states = states.reshape(2, 2 * count, 2 * SIDE)

    own_all_p = swapped(own_all, "core")
    other_main, own_all_p, _ = lax.optimization_barrier((other_main, own_all_p, partner))
    other_main_p = swapped(other_main, "core")
    scale = jnp.repeat(cosine_logit_scale, HEAD)[None, :]
    weights = (own_all, other_main, own_all_p, other_main_p)
    size = 2 * count
    grid = np.arange(size).reshape(2, 2, members, rows, HALF)
    order = one_hot(grid.transpose(3, 1, 0, 2, 4).reshape(-1), size)
    latent = front_latents(flags, states, weights, scale, order)
    tables, latent, own_all, own_all_p = lax.optimization_barrier(
        (both[:, count:], latent, own_all, own_all_p)
    )
    obs = weighted_places(in_order(zh, tables[:1], tables[1:], 0), sensor_gridpoint.size)
    moved = exchanged(latent.reshape(16, size // 16, width)).reshape(size, width)

    grid = np.arange(size).reshape(16, 2, members, HALF)
    order = one_hot(grid.transpose(3, 1, 0, 2).reshape(-1), size)
    grid = np.arange(count).reshape(HALF, 16, members)
    back_order = one_hot(grid.transpose(1, 2, 0).reshape(-1), count)
    posterior = analysis(flags, moved, order, back_order, obs, other_main, other_main_p)
    back = exchanged(posterior.reshape(16, count // 16, width)).reshape(count, width)

    def strip(own, other):
        own, other = own[:, None, o_end : o_end + SHARD], other[:, None, o_end : o_end + SHARD]
        return in_order(zh, own, other, 1).reshape(feats, -1)

    grid = np.arange(count).reshape(rows, 2, members, HALF)
    order = one_hot(grid.transpose(2, 0, 1, 3).reshape(-1), count)
    result = decode(
        flags,
        back,
        order,
        strip(own_all, other_main),
        strip(own_all_p, other_main_p),
    )
    return result.reshape(members, rows, cols, feats)


def solution(mesh):
    fine = Mesh(
        np.asarray(mesh.devices).reshape(4, 4, 2, 8, 2), ("x", "y", "zh", "zl", "core")
    )
    return jax.shard_map(
        per_device,
        mesh=fine,
        in_specs=(
            P(MEM, None, TILE, None),
            P(MEM, None),
            P(None, MEM),
            P(None, MEM),
            P(None, MEM),
            P(),
            P(),
            P(MEM, TILE, None),
            P(MEM, TILE, None),
            P(MEM, TILE, None),
            P(MEM, TILE, None),
            P(MEM, TILE, None),
        ),
        out_specs=P(MEM, None, TILE, None),
        check_vma=False,
    )
```

```python
import functools

import numpy as np
import jax
import jax.numpy as jnp
from jax import lax
from jax.experimental import pallas as pl
from jax.experimental.pallas import tpu as pltpu
from jax.sharding import Mesh, PartitionSpec as P

PANE_SIDE = 8
HALF = PANE_SIDE // 2
NS_ITERS = 5
PLANE = ("x", "y")
MEM = ("x", "y", "zh")
TILE = ("zl", "core")
BLOCK = 40
SHARD = 35
SIDE = 16 * BLOCK
HEAD = 64
GROUP = 4 * HEAD
OWN = PANE_SIDE * HALF

eps_norm = 1e-05
normalizing_guard = 1e-06
bf16 = jnp.bfloat16
f32 = jnp.float32


def swapped(value, axis):
    return lax.ppermute(value, axis, [(0, 1), (1, 0)])


def shifted(value, by):
    return lax.ppermute(value, ("zh", "zl"), [(z, (z + by) % 16) for z in range(16)])


def crossed(value):
    pairs = [(8 * h + z, 8 * (1 - h) + (z + 4) % 8) for h in range(2) for z in range(8)]
    return lax.ppermute(value, ("zh", "zl"), pairs)


def between_chips(value):
    pairs = [(2 * z, 2 * ((z - 1) % 8) + 1) for z in range(8)]
    return lax.ppermute(value, TILE, pairs + [(b, a) for a, b in pairs])


def copies_of(part):
    return lax.optimization_barrier(jnp.broadcast_to(part[None], (16,) + part.shape))


def exchanged(blocks):
    return lax.all_to_all(blocks, PLANE, split_axis=0, concat_axis=0, tiled=True)


def times(left, right):
    return jnp.dot(left, right, preferred_element_type=f32)


def times_t(left, right):
    return lax.dot_general(left, right, (((1,), (1,)), ((), ())), preferred_element_type=f32)


def normalized(values):
    center = values - jnp.mean(values, axis=-1, keepdims=True)
    spread = jnp.mean(center * center, axis=-1, keepdims=True)
    return center * lax.rsqrt(spread + eps_norm)


def in_order(flag, first, second, axis):
    low = jnp.where(flag == 0, first, second)
    high = jnp.where(flag == 0, second, first)
    return jnp.concatenate([low, high], axis=axis)


def halves(flag, value):
    width = value.shape[-1] // 2
    low, high = value[..., :width], value[..., width:]
    return jnp.where(flag == 0, low, high), jnp.where(flag == 0, high, low)


def two_parts(value):
    high = value.astype(bf16)
    return high, (value - high.astype(f32)).astype(bf16)


def three_parts(value):
    high = value.astype(bf16)
    rest = value - high.astype(f32)
    middle = rest.astype(bf16)
    return high, middle, (rest - middle.astype(f32)).astype(bf16)


def iota(shape, axis):
    return lax.broadcasted_iota(jnp.int32, shape, axis)


def one_hot(order, width):
    return jnp.asarray(np.asarray(order)[:, None] == np.arange(width)[None, :], bf16)


def front_kernel(
    flags,
    x_all,
    own_m,
    other_m,
    own_p,
    other_p,
    scale,
    order,
    latent_out,
    w_mine,
    w_part,
):
    core, zh = flags[0], flags[1]
    lanes = own_m.shape[2]
    lifts, outs = 6 * lanes // 32, 2 * lanes // 32
    front = lifts + BLOCK
    width = 2 * lanes

    for target, own, other in ((w_mine, own_m, other_m), (w_part, own_p, other_p)):
        for place in range(16):
            target[2 * lifts * place : 2 * lifts * (place + 1), :] = in_order(
                zh, own[place, :lifts, :], other[place, :lifts, :], 0
            )

    def embed(own, other):
        return times(x_own, own[:, lifts:front, :].reshape(SIDE, lanes)) + times(
            x_other, other[:, lifts:front, :].reshape(SIDE, lanes)
        )

    groups, count = x_all.shape[0], x_all.shape[1] // 2
    x = jnp.concatenate(
        [x_all[g, i * count : (i + 1) * count, :] for i in range(2) for g in range(groups)], axis=0
    )
    x_own, x_other = halves(zh, x)
    hidden = in_order(core, embed(own_m, other_m), embed(own_p, other_p), 1).astype(bf16)
    normed = normalized(hidden.astype(f32)).astype(bf16)
    n_mine, n_part = halves(core, normed)
    own_rows = groups * count

    same = (iota((GROUP, GROUP), 0) // HEAD) == (iota((GROUP, GROUP), 1) // HEAD)
    ones = same.astype(bf16)
    lane_head = iota((PANE_SIDE * PANE_SIDE, GROUP), 1) // HEAD

    def projected(left, right, start):
        rows = pl.ds(start, GROUP)
        return (times_t(left, w_mine[rows, :]) + times_t(right, w_part[rows, :])).astype(bf16)

    def unit(values):
        total = times(values * values, ones)
        values = values.astype(f32)
        return (values * lax.rsqrt(total + normalizing_guard)).astype(bf16)

    def diagonal(rows):
        zero = jnp.zeros_like(rows)
        return jnp.concatenate([jnp.where(lane_head == h, rows, zero) for h in range(4)], axis=0)

    def pane_rows(values, i):
        return jnp.concatenate(
            [values[i * OWN : (i + 1) * OWN], values[own_rows + i * OWN :][:OWN]], axis=0
        )

    panes = own_rows // OWN
    context = []
    for g in range(width // GROUP):
        at = g * GROUP
        query = unit(projected(n_mine[:own_rows], n_part[:own_rows], at))
        key_rows = unit(projected(n_mine, n_part, width + at))
        value_rows = projected(n_mine, n_part, 2 * width + at)
        scores = [
            times_t(query[i * OWN : (i + 1) * OWN], diagonal(pane_rows(key_rows, i)))
            for i in range(panes)
        ]
        weights = jnp.exp(jnp.concatenate(scores, axis=0) * scale[:, at : at + GROUP]).astype(bf16)
        total = times(weights, ones)
        mixed = [
            times(weights[i * OWN : (i + 1) * OWN], diagonal(pane_rows(value_rows, i)))
            for i in range(panes)
        ]
        context.append((jnp.concatenate(mixed, axis=0) / total).astype(bf16))
    c_mine, c_part = halves(core, jnp.concatenate(context, axis=1))

    def combiner(own, other):
        rows = [
            in_order(
                zh, own[place, front : front + outs, :], other[place, front : front + outs, :], 0
            )
            for place in range(16)
        ]
        return jnp.concatenate(rows, axis=0)

    mixed = times_t(c_mine, combiner(own_m, other_m)) + times_t(c_part, combiner(own_p, other_p))
    latent = normalized(hidden[:own_rows].astype(f32) + mixed).astype(bf16)
    latent_out[...] = times(order[...], latent).astype(bf16)


def front_latents(flags, states, weights, scale, order):
    lanes = weights[0].shape[2]
    vmem = pl.BlockSpec(memory_space=pltpu.VMEM)
    return pl.pallas_call(
        front_kernel,
        in_specs=[pl.BlockSpec(memory_space=pltpu.SMEM)] + [vmem] * (3 + len(weights)),
        out_specs=vmem,
        out_shape=jax.ShapeDtypeStruct((order.shape[0], 2 * lanes), bf16),
        scratch_shapes=[pltpu.VMEM((6 * lanes, lanes), bf16)] * 2,
        compiler_params=pltpu.CompilerParams(vmem_limit_bytes=16 * 1024 * 1024),
        name="front",
    )(flags, states, *weights, scale, order)


def prepare_kernel(x, order, grid, domain, channel, reading, noise, packed):
    count = x.shape[0]
    packed[:count, :] = times(order[...], x[...]).astype(bf16)
    table = [grid[...].astype(f32), domain[...].astype(f32), channel[...].astype(f32)]
    table = [t.astype(bf16) for t in table]
    table += list(three_parts(reading[...])) + list(three_parts(noise[...]))
    table = jnp.concatenate([t.astype(f32) for t in table], axis=0)
    packed[count:, :] = jnp.zeros((16, packed.shape[1]), bf16)
    table = jnp.concatenate([table, jnp.zeros((16 - table.shape[0], table.shape[1]), f32)], axis=0)
    packed[count:, : table.shape[1]] = table.astype(bf16)


def prepare(x, order, *obs):
    vmem = pl.BlockSpec(memory_space=pltpu.VMEM)
    count, feats = x.shape
    return pl.pallas_call(
        prepare_kernel,
        in_specs=[vmem] * (2 + len(obs)),
        out_specs=vmem,
        out_shape=jax.ShapeDtypeStruct((count + 16, feats), bf16),
        name="prepare",
    )(x, order, *obs)


def product(left, right):
    l_high, l_low = two_parts(left)
    r_high, r_low = two_parts(right)
    return times(
        jnp.concatenate([l_high, l_high, l_low], axis=1),
        jnp.concatenate([r_high, r_low, r_high], axis=0),
    )


def product_t(left, right):
    l_high, l_low = two_parts(left)
    r_high, r_low = two_parts(right)
    return times_t(
        jnp.concatenate([l_high, l_high, l_low], axis=1),
        jnp.concatenate([r_high, r_low, r_high], axis=1),
    )


def analysis_kernel(flags, moved, order, back_order, obs, t_mine, t_part, posterior_out):
    latent = times(order[...], moved[...]).astype(bf16)
    members = latent.shape[0] // HALF
    l_mine, l_part = halves(flags[0], latent)

    def readers(ref):
        return ref[:, ref.shape[1] - 16 :, :].reshape(16 * 16, ref.shape[2])

    seen = times_t(l_mine, readers(t_mine)) + times_t(l_part, readers(t_part))
    eye = (iota((members, members), 0) == iota((members, members), 1)).astype(f32)
    systems, drives = [], []
    for block in range(2):
        ens = [seen[(2 * block + t) * members : (2 * block + t + 1) * members] for t in range(2)]
        mean = [jnp.mean(e, axis=0, keepdims=True) for e in ens]
        pert = jnp.concatenate([e - m for e, m in zip(ens, mean)], axis=1)
        mean = jnp.concatenate(mean, axis=1)
        for r in range(2):
            weight = obs[block, r : r + 1, :]
            read = obs[block, 2 + r : 3 + r, :]
            gram = product_t(pert * weight, pert)
            drives.append(jnp.sum(pert * (read - weight * mean), axis=1, keepdims=True))
            systems.append(eye + gram / (members - 1.0))
    bounds = [
        jnp.max(jnp.sum(jnp.abs(s), axis=1, keepdims=True), axis=0, keepdims=True) for s in systems
    ]
    iterates = [s / b for s, b in zip(systems, bounds)]
    factors = [1.5 * eye - 0.5 * y for y in iterates]
    iterates = [product(y, f) for y, f in zip(iterates, factors)]
    roots = factors
    for step in range(1, NS_ITERS):
        factors = [1.5 * eye - 0.5 * product(z, y) for z, y in zip(roots, iterates)]
        if step + 1 < NS_ITERS:
            iterates = [product(y, f) for y, f in zip(iterates, factors)]
        roots = [product(f, z) for f, z in zip(factors, roots)]
    results = []
    for region in range(2 * 2):
        root = roots[region] * lax.rsqrt(bounds[region])
        inner = jnp.sum(root * drives[region], axis=0, keepdims=True)
        mean_weight = jnp.sum(root * inner, axis=1, keepdims=True) / (members - 1.0)
        transform = root + mean_weight
        own_t = transform[:, : members // 2].T
        values = latent[region * members : (region + 1) * members]
        center = jnp.mean(values.astype(f32), axis=0, keepdims=True)
        high, middle, low = three_parts(own_t)
        left = jnp.concatenate([high, middle, low], axis=1)
        moved_part = times(left, jnp.concatenate([values] * 3, axis=0))
        share = 1.0 - jnp.sum(own_t, axis=1, keepdims=True)
        results.append((moved_part + share * center).astype(bf16))
    posterior = jnp.concatenate(results, axis=0)
    posterior_out[...] = times(back_order[...], posterior).astype(bf16)


def analysis(flags, moved, order, back_order, obs, t_mine, t_part):
    vmem = pl.BlockSpec(memory_space=pltpu.VMEM)
    return pl.pallas_call(
        analysis_kernel,
        in_specs=[pl.BlockSpec(memory_space=pltpu.SMEM)] + [vmem] * 6,
        out_specs=vmem,
        out_shape=jax.ShapeDtypeStruct((back_order.shape[0], moved.shape[1]), bf16),
        compiler_params=pltpu.CompilerParams(vmem_limit_bytes=12 * 1024 * 1024),
        name="analysis",
    )(flags, moved, order, back_order, obs, t_mine, t_part)


def decode_kernel(flags, parts, order, d_mine, d_part, out):
    b_mine, b_part = halves(flags[0], times(order[...], parts[...]).astype(bf16))
    out[...] = (times_t(b_mine, d_mine[...]) + times_t(b_part, d_part[...])).astype(bf16)


def decode(flags, parts, order, d_mine, d_part):
    vmem = pl.BlockSpec(memory_space=pltpu.VMEM)
    return pl.pallas_call(
        decode_kernel,
        in_specs=[pl.BlockSpec(memory_space=pltpu.SMEM)] + [vmem] * 4,
        out_specs=vmem,
        out_shape=jax.ShapeDtypeStruct((order.shape[0], d_mine.shape[0]), bf16),
        compiler_params=pltpu.CompilerParams(vmem_limit_bytes=12 * 1024 * 1024),
        name="decode",
    )(flags, parts, order, d_mine, d_part)


def weighted_places(table, count):
    table = table[:, :, :count].astype(f32)
    grid = table[:, 0].astype(jnp.int32)
    domain = table[:, 1].astype(jnp.int32)
    channel = table[:, 2].astype(jnp.int32)
    reading = table[:, 3] + (table[:, 4] + table[:, 5])
    noise = table[:, 6] + (table[:, 7] + table[:, 8])
    token = grid // 16
    distance = (token - domain).astype(f32)
    weight = jnp.exp(-0.5 * distance * distance) / (noise * noise)
    region = (domain[:, None, :] == jnp.arange(2, dtype=jnp.int32)[None, :, None]).astype(f32)
    weight = region * weight[:, None, :]
    left = jnp.concatenate([weight, weight * reading[:, None, :]], axis=1)
    place = grid * 16 + channel
    pick = (place[:, :, None] == jnp.arange(512, dtype=jnp.int32)[None, None, :]).astype(f32)
    return jnp.einsum("bcj,bjp->bcp", left, pick, precision=lax.Precision.HIGHEST)


def per_device(
    starting_ensemble,
    patch_lifting,
    query_keyvalue_lift,
    output_combiner,
    decoder_linear_map,
    cosine_logit_scale,
    sensor_variable_loadings,
    sensor_gridpoint,
    sensor_domain_index,
    sensor_channel_list,
    sensor_reading,
    sensor_noise_deviation,
):
    members, rows, cols, feats = starting_ensemble.shape
    width = patch_lifting.shape[1]
    core = lax.axis_index("core")
    zh = lax.axis_index("zh")
    flags = jnp.stack([core, zh]).astype(jnp.int32)

    fill = ((0, BLOCK - SHARD), (0, 0))
    packed = jnp.concatenate(
        [
            query_keyvalue_lift.T,
            jnp.pad(patch_lifting, fill),
            output_combiner.T,
            jnp.pad(decoder_linear_map.T, fill),
        ],
        axis=0,
    )
    mine, _ = halves(core, packed)
    lanes = mine.shape[1]
    front = query_keyvalue_lift.shape[1] + BLOCK
    o_end = front + output_combiner.shape[1]
    own_all = exchanged(copies_of(mine))

    count = members * rows * cols
    grid = np.arange(count).reshape(members, rows, 2, HALF)
    pick_rows = one_hot(grid.transpose(2, 0, 1, 3).reshape(-1), count)
    obs = (
        sensor_gridpoint,
        sensor_domain_index,
        sensor_channel_list,
        sensor_reading,
        sensor_noise_deviation,
    )
    sent = prepare(
        starting_ensemble.reshape(count, feats), pick_rows, *(o.reshape(1, -1) for o in obs)
    )
    sent, outgoing = lax.optimization_barrier((sent, mine))
    theirs = crossed(outgoing)
    middle = (count + 16) // 2
    up, down = shifted(sent[:middle], 4), shifted(sent[middle:], -4)

    decoder = in_order(zh, mine[o_end:], theirs[o_end:], 0)
    loadings = jnp.pad(
        sensor_variable_loadings.reshape(16, 2, SHARD), ((0, 0), (0, 0), (0, BLOCK - SHARD))
    ).reshape(16, 2 * BLOCK)
    readers = times(loadings, decoder).astype(bf16)
    copies, own_all = lax.optimization_barrier(
        (copies_of(jnp.concatenate([theirs, readers], axis=0)), own_all)
    )
    up, down, own_sent = lax.optimization_barrier((up, down, own_all))
    partner = jnp.concatenate([shifted(up, 4), shifted(down, -4)], axis=0)
    other_main = exchanged(copies)
    inside = np.arange(BLOCK)[None, None, :]
    place = np.arange(16)[None, :, None] * 2 + np.arange(2)[:, None, None]
    source = np.where(inside < SHARD, place * SHARD + inside, -1).reshape(-1)
    pick_cols = jnp.asarray(np.arange(feats)[:, None] == source[None, :], bf16)

    both = jnp.stack([sent, partner])
    low, high = both[:, : count // 2], both[:, count // 2 : count]
    core_x = swapped(jnp.where(core == 0, high, low), "core")
    chip_x = between_chips(jnp.where(core == 0, low, high))

    states = jnp.concatenate([both[:, :count], in_order(core, chip_x, core_x, 1)], axis=1)
    states = times(states.reshape(4 * count, feats), pick_cols).astype(bf16)
    states = states.reshape(2, 2 * count, 2 * SIDE)

    own_all_p = swapped(own_sent, "core")
    other_main, own_all_p, _ = lax.optimization_barrier((other_main, own_all_p, partner))
    other_main_p = swapped(other_main, "core")
    scale = jnp.repeat(cosine_logit_scale, HEAD)[None, :]
    weights = (own_all, other_main, own_all_p, other_main_p)
    size = 2 * count
    grid = np.arange(size).reshape(2, 2, members, rows, HALF)
    order = one_hot(grid.transpose(3, 1, 0, 2, 4).reshape(-1), size)
    latent = front_latents(flags, states, weights, scale, order)
    tables, latent, own_all, own_all_p = lax.optimization_barrier(
        (both[:, count:], latent, own_all, own_all_p)
    )
    obs = weighted_places(in_order(zh, tables[:1], tables[1:], 0), sensor_gridpoint.size)
    moved = exchanged(latent.reshape(16, size // 16, width)).reshape(size, width)

    grid = np.arange(size).reshape(16, 2, members, HALF)
    order = one_hot(grid.transpose(3, 1, 0, 2).reshape(-1), size)
    grid = np.arange(count).reshape(HALF, 16, members)
    back_order = one_hot(grid.transpose(1, 2, 0).reshape(-1), count)
    posterior = analysis(flags, moved, order, back_order, obs, other_main, other_main_p)
    back = exchanged(posterior.reshape(16, count // 16, width)).reshape(count, width)

    def strip(own, other):
        own, other = own[:, None, o_end : o_end + SHARD], other[:, None, o_end : o_end + SHARD]
        return in_order(zh, own, other, 1).reshape(feats, -1)

    grid = np.arange(count).reshape(rows, 2, members, HALF)
    order = one_hot(grid.transpose(2, 0, 1, 3).reshape(-1), count)
    result = decode(
        flags,
        back,
        order,
        strip(own_all, other_main),
        strip(own_all_p, other_main_p),
    )
    return result.reshape(members, rows, cols, feats)


def solution(mesh):
    fine = Mesh(
        np.asarray(mesh.devices).reshape(4, 4, 2, 8, 2), ("x", "y", "zh", "zl", "core")
    )
    return jax.shard_map(
        per_device,
        mesh=fine,
        in_specs=(
            P(MEM, None, TILE, None),
            P(MEM, None),
            P(None, MEM),
            P(None, MEM),
            P(None, MEM),
            P(),
            P(),
            P(MEM, TILE, None),
            P(MEM, TILE, None),
            P(MEM, TILE, None),
            P(MEM, TILE, None),
            P(MEM, TILE, None),
        ),
        out_specs=P(MEM, None, TILE, None),
        check_vma=False,
    )
```

```python
import functools

import numpy as np
import jax
import jax.numpy as jnp
from jax import lax
from jax.experimental import pallas as pl
from jax.experimental.pallas import tpu as pltpu
from jax.sharding import Mesh, PartitionSpec as P

PANE_SIDE = 8
HALF = PANE_SIDE // 2
NS_ITERS = 5
PLANE = ("x", "y")
MEM = ("x", "y", "zh")
TILE = ("zl", "core")
BLOCK = 40
SHARD = 35
SIDE = 16 * BLOCK
HEAD = 64
GROUP = 4 * HEAD
OWN = PANE_SIDE * HALF

eps_norm = 1e-05
normalizing_guard = 1e-06
bf16 = jnp.bfloat16
f32 = jnp.float32


def swapped(value, axis):
    return lax.ppermute(value, axis, [(0, 1), (1, 0)])


def shifted(value, by):
    return lax.ppermute(value, ("zh", "zl"), [(z, (z + by) % 16) for z in range(16)])


def crossed(value):
    pairs = [(z, 15 - z) for z in range(16)]
    return lax.ppermute(value, ("zh", "zl"), pairs)


def between_chips(value):
    pairs = [(2 * z, 2 * ((z - 1) % 8) + 1) for z in range(8)]
    return lax.ppermute(value, TILE, pairs + [(b, a) for a, b in pairs])


def copies_of(part):
    return lax.optimization_barrier(jnp.broadcast_to(part[None], (16,) + part.shape))


def exchanged(blocks):
    return lax.all_to_all(blocks, PLANE, split_axis=0, concat_axis=0, tiled=True)


def times(left, right):
    return jnp.dot(left, right, preferred_element_type=f32)


def times_t(left, right):
    return lax.dot_general(left, right, (((1,), (1,)), ((), ())), preferred_element_type=f32)


def normalized(values):
    center = values - jnp.mean(values, axis=-1, keepdims=True)
    spread = jnp.mean(center * center, axis=-1, keepdims=True)
    return center * lax.rsqrt(spread + eps_norm)


def in_order(flag, first, second, axis):
    low = jnp.where(flag == 0, first, second)
    high = jnp.where(flag == 0, second, first)
    return jnp.concatenate([low, high], axis=axis)


def halves(flag, value):
    width = value.shape[-1] // 2
    low, high = value[..., :width], value[..., width:]
    return jnp.where(flag == 0, low, high), jnp.where(flag == 0, high, low)


def two_parts(value):
    high = value.astype(bf16)
    return high, (value - high.astype(f32)).astype(bf16)


def three_parts(value):
    high = value.astype(bf16)
    rest = value - high.astype(f32)
    middle = rest.astype(bf16)
    return high, middle, (rest - middle.astype(f32)).astype(bf16)


def iota(shape, axis):
    return lax.broadcasted_iota(jnp.int32, shape, axis)


def one_hot(order, width):
    return jnp.asarray(np.asarray(order)[:, None] == np.arange(width)[None, :], bf16)


def front_kernel(
    flags,
    x_all,
    own_m,
    other_m,
    own_p,
    other_p,
    scale,
    order,
    latent_out,
    w_mine,
    w_part,
):
    core, zh = flags[0], flags[1]
    lanes = own_m.shape[2]
    lifts, outs = 6 * lanes // 32, 2 * lanes // 32
    front = lifts + BLOCK
    width = 2 * lanes

    for target, own, other in ((w_mine, own_m, other_m), (w_part, own_p, other_p)):
        for place in range(16):
            target[2 * lifts * place : 2 * lifts * (place + 1), :] = in_order(
                zh, own[place, :lifts, :], other[place, :lifts, :], 0
            )

    def embed(own, other):
        return times(x_own, own[:, lifts:front, :].reshape(SIDE, lanes)) + times(
            x_other, other[:, lifts:front, :].reshape(SIDE, lanes)
        )

    groups, count = x_all.shape[0], x_all.shape[1] // 2
    x = jnp.concatenate(
        [x_all[g, i * count : (i + 1) * count, :] for i in range(2) for g in range(groups)], axis=0
    )
    x_own, x_other = halves(zh, x)
    hidden = in_order(core, embed(own_m, other_m), embed(own_p, other_p), 1).astype(bf16)
    normed = normalized(hidden.astype(f32)).astype(bf16)
    n_mine, n_part = halves(core, normed)
    own_rows = groups * count

    same = (iota((GROUP, GROUP), 0) // HEAD) == (iota((GROUP, GROUP), 1) // HEAD)
    ones = same.astype(bf16)
    lane_head = iota((PANE_SIDE * PANE_SIDE, GROUP), 1) // HEAD

    def projected(left, right, start):
        rows = pl.ds(start, GROUP)
        return (times_t(left, w_mine[rows, :]) + times_t(right, w_part[rows, :])).astype(bf16)

    def unit(values):
        total = times(values * values, ones)
        values = values.astype(f32)
        return (values * lax.rsqrt(total + normalizing_guard)).astype(bf16)

    def diagonal(rows):
        zero = jnp.zeros_like(rows)
        return jnp.concatenate([jnp.where(lane_head == h, rows, zero) for h in range(4)], axis=0)

    def pane_rows(values, i):
        return jnp.concatenate(
            [values[i * OWN : (i + 1) * OWN], values[own_rows + i * OWN :][:OWN]], axis=0
        )

    panes = own_rows // OWN
    context = []
    for g in range(width // GROUP):
        at = g * GROUP
        query = unit(projected(n_mine[:own_rows], n_part[:own_rows], at))
        key_rows = unit(projected(n_mine, n_part, width + at))
        value_rows = projected(n_mine, n_part, 2 * width + at)
        scores = [
            times_t(query[i * OWN : (i + 1) * OWN], diagonal(pane_rows(key_rows, i)))
            for i in range(panes)
        ]
        weights = jnp.exp(jnp.concatenate(scores, axis=0) * scale[:, at : at + GROUP]).astype(bf16)
        total = times(weights, ones)
        mixed = [
            times(weights[i * OWN : (i + 1) * OWN], diagonal(pane_rows(value_rows, i)))
            for i in range(panes)
        ]
        context.append((jnp.concatenate(mixed, axis=0) / total).astype(bf16))
    c_mine, c_part = halves(core, jnp.concatenate(context, axis=1))

    def combiner(own, other):
        rows = [
            in_order(
                zh, own[place, front : front + outs, :], other[place, front : front + outs, :], 0
            )
            for place in range(16)
        ]
        return jnp.concatenate(rows, axis=0)

    mixed = times_t(c_mine, combiner(own_m, other_m)) + times_t(c_part, combiner(own_p, other_p))
    latent = normalized(hidden[:own_rows].astype(f32) + mixed).astype(bf16)
    latent_out[...] = times(order[...], latent).astype(bf16)


def front_latents(flags, states, weights, scale, order):
    lanes = weights[0].shape[2]
    vmem = pl.BlockSpec(memory_space=pltpu.VMEM)
    return pl.pallas_call(
        front_kernel,
        in_specs=[pl.BlockSpec(memory_space=pltpu.SMEM)] + [vmem] * (3 + len(weights)),
        out_specs=vmem,
        out_shape=jax.ShapeDtypeStruct((order.shape[0], 2 * lanes), bf16),
        scratch_shapes=[pltpu.VMEM((6 * lanes, lanes), bf16)] * 2,
        compiler_params=pltpu.CompilerParams(vmem_limit_bytes=16 * 1024 * 1024),
        name="front",
    )(flags, states, *weights, scale, order)


def prepare_kernel(x, order, grid, domain, channel, reading, noise, packed):
    count = x.shape[0]
    packed[:count, :] = times(order[...], x[...]).astype(bf16)
    table = [grid[...].astype(f32), domain[...].astype(f32), channel[...].astype(f32)]
    table = [t.astype(bf16) for t in table]
    table += list(three_parts(reading[...])) + list(three_parts(noise[...]))
    table = jnp.concatenate([t.astype(f32) for t in table], axis=0)
    packed[count:, :] = jnp.zeros((16, packed.shape[1]), bf16)
    table = jnp.concatenate([table, jnp.zeros((16 - table.shape[0], table.shape[1]), f32)], axis=0)
    packed[count:, : table.shape[1]] = table.astype(bf16)


def prepare(x, order, *obs):
    vmem = pl.BlockSpec(memory_space=pltpu.VMEM)
    count, feats = x.shape
    return pl.pallas_call(
        prepare_kernel,
        in_specs=[vmem] * (2 + len(obs)),
        out_specs=vmem,
        out_shape=jax.ShapeDtypeStruct((count + 16, feats), bf16),
        name="prepare",
    )(x, order, *obs)


def product(left, right):
    l_high, l_low = two_parts(left)
    r_high, r_low = two_parts(right)
    return times(
        jnp.concatenate([l_high, l_high, l_low], axis=1),
        jnp.concatenate([r_high, r_low, r_high], axis=0),
    )


def product_t(left, right):
    l_high, l_low = two_parts(left)
    r_high, r_low = two_parts(right)
    return times_t(
        jnp.concatenate([l_high, l_high, l_low], axis=1),
        jnp.concatenate([r_high, r_low, r_high], axis=1),
    )


def analysis_kernel(flags, moved, order, back_order, obs, r_mine, r_part, posterior_out):
    latent = times(order[...], moved[...]).astype(bf16)
    members = latent.shape[0] // HALF
    l_mine, l_part = halves(flags[0], latent)

    seen = times_t(l_mine, r_mine[...]) + times_t(l_part, r_part[...])
    eye = (iota((members, members), 0) == iota((members, members), 1)).astype(f32)
    systems, drives = [], []
    for block in range(2):
        ens = [seen[(2 * block + t) * members : (2 * block + t + 1) * members] for t in range(2)]
        mean = [jnp.mean(e, axis=0, keepdims=True) for e in ens]
        pert = jnp.concatenate([e - m for e, m in zip(ens, mean)], axis=1)
        mean = jnp.concatenate(mean, axis=1)
        for r in range(2):
            weight = obs[block, r : r + 1, :]
            read = obs[block, 2 + r : 3 + r, :]
            gram = product_t(pert * weight, pert)
            drives.append(jnp.sum(pert * (read - weight * mean), axis=1, keepdims=True))
            systems.append(eye + gram / (members - 1.0))
    bounds = [
        jnp.max(jnp.sum(jnp.abs(s), axis=1, keepdims=True), axis=0, keepdims=True) for s in systems
    ]
    iterates = [s / b for s, b in zip(systems, bounds)]
    factors = [1.5 * eye - 0.5 * y for y in iterates]
    iterates = [product(y, f) for y, f in zip(iterates, factors)]
    roots = factors
    for step in range(1, NS_ITERS):
        factors = [1.5 * eye - 0.5 * product(z, y) for z, y in zip(roots, iterates)]
        if step + 1 < NS_ITERS:
            iterates = [product(y, f) for y, f in zip(iterates, factors)]
        roots = [product(f, z) for f, z in zip(factors, roots)]
    results = []
    for region in range(2 * 2):
        root = roots[region] * lax.rsqrt(bounds[region])
        inner = jnp.sum(root * drives[region], axis=0, keepdims=True)
        mean_weight = jnp.sum(root * inner, axis=1, keepdims=True) / (members - 1.0)
        transform = root + mean_weight
        own_t = transform[:, : members // 2].T
        values = latent[region * members : (region + 1) * members]
        center = jnp.mean(values.astype(f32), axis=0, keepdims=True)
        high, middle, low = three_parts(own_t)
        left = jnp.concatenate([high, middle, low], axis=1)
        moved_part = times(left, jnp.concatenate([values] * 3, axis=0))
        share = 1.0 - jnp.sum(own_t, axis=1, keepdims=True)
        results.append((moved_part + share * center).astype(bf16))
    posterior = jnp.concatenate(results, axis=0)
    posterior_out[...] = times(back_order[...], posterior).astype(bf16)


def analysis(flags, moved, order, back_order, obs, r_mine, r_part):
    vmem = pl.BlockSpec(memory_space=pltpu.VMEM)
    return pl.pallas_call(
        analysis_kernel,
        in_specs=[pl.BlockSpec(memory_space=pltpu.SMEM)] + [vmem] * 6,
        out_specs=vmem,
        out_shape=jax.ShapeDtypeStruct((back_order.shape[0], moved.shape[1]), bf16),
        compiler_params=pltpu.CompilerParams(vmem_limit_bytes=12 * 1024 * 1024),
        name="analysis",
    )(flags, moved, order, back_order, obs, r_mine, r_part)


def decode_kernel(flags, parts, order, d_mine, d_part, out):
    b_mine, b_part = halves(flags[0], times(order[...], parts[...]).astype(bf16))
    out[...] = (times_t(b_mine, d_mine[...]) + times_t(b_part, d_part[...])).astype(bf16)


def decode(flags, parts, order, d_mine, d_part):
    vmem = pl.BlockSpec(memory_space=pltpu.VMEM)
    return pl.pallas_call(
        decode_kernel,
        in_specs=[pl.BlockSpec(memory_space=pltpu.SMEM)] + [vmem] * 4,
        out_specs=vmem,
        out_shape=jax.ShapeDtypeStruct((order.shape[0], d_mine.shape[0]), bf16),
        compiler_params=pltpu.CompilerParams(vmem_limit_bytes=12 * 1024 * 1024),
        name="decode",
    )(flags, parts, order, d_mine, d_part)


def weighted_places(table, count):
    table = table[:, :, :count].astype(f32)
    grid = table[:, 0].astype(jnp.int32)
    domain = table[:, 1].astype(jnp.int32)
    channel = table[:, 2].astype(jnp.int32)
    reading = table[:, 3] + (table[:, 4] + table[:, 5])
    noise = table[:, 6] + (table[:, 7] + table[:, 8])
    token = grid // 16
    distance = (token - domain).astype(f32)
    weight = jnp.exp(-0.5 * distance * distance) / (noise * noise)
    region = (domain[:, None, :] == jnp.arange(2, dtype=jnp.int32)[None, :, None]).astype(f32)
    weight = region * weight[:, None, :]
    left = jnp.concatenate([weight, weight * reading[:, None, :]], axis=1)
    place = grid * 16 + channel
    pick = (place[:, :, None] == jnp.arange(512, dtype=jnp.int32)[None, None, :]).astype(f32)
    return jnp.einsum("bcj,bjp->bcp", left, pick, precision=lax.Precision.HIGHEST)


def per_device(
    starting_ensemble,
    patch_lifting,
    query_keyvalue_lift,
    output_combiner,
    decoder_linear_map,
    cosine_logit_scale,
    sensor_variable_loadings,
    sensor_gridpoint,
    sensor_domain_index,
    sensor_channel_list,
    sensor_reading,
    sensor_noise_deviation,
):
    members, rows, cols, feats = starting_ensemble.shape
    width = patch_lifting.shape[1]
    core = lax.axis_index("core")
    zh = lax.axis_index("zh")
    flags = jnp.stack([core, zh]).astype(jnp.int32)

    fill = ((0, BLOCK - SHARD), (0, 0))
    packed = jnp.concatenate(
        [
            query_keyvalue_lift.T,
            jnp.pad(patch_lifting, fill),
            output_combiner.T,
            jnp.pad(decoder_linear_map.T, fill),
        ],
        axis=0,
    )
    mine, _ = halves(core, packed)
    lanes = mine.shape[1]
    front = query_keyvalue_lift.shape[1] + BLOCK
    o_end = front + output_combiner.shape[1]
    own_all = exchanged(copies_of(mine))

    count = members * rows * cols
    grid = np.arange(count).reshape(members, rows, 2, HALF)
    pick_rows = one_hot(grid.transpose(2, 0, 1, 3).reshape(-1), count)
    obs = (
        sensor_gridpoint,
        sensor_domain_index,
        sensor_channel_list,
        sensor_reading,
        sensor_noise_deviation,
    )
    sent = prepare(
        starting_ensemble.reshape(count, feats), pick_rows, *(o.reshape(1, -1) for o in obs)
    )
    sent, outgoing = lax.optimization_barrier((sent, mine))
    theirs = crossed(outgoing)
    middle = (count + 16) // 2
    up, down = shifted(sent[:middle], 4), shifted(sent[middle:], -4)

    decoder = in_order(zh, mine[o_end:], theirs[o_end:], 0)
    loadings = jnp.pad(
        sensor_variable_loadings.reshape(16, 2, SHARD), ((0, 0), (0, 0), (0, BLOCK - SHARD))
    ).reshape(16, 2 * BLOCK)
    readers = times(loadings, decoder).astype(bf16)
    copies, own_all = lax.optimization_barrier(
        (copies_of(jnp.concatenate([theirs, readers], axis=0)), own_all)
    )
    up, down, own_sent = lax.optimization_barrier((up, down, own_all))
    partner = jnp.concatenate([shifted(up, 4), shifted(down, -4)], axis=0)
    other_main = exchanged(copies)
    inside = np.arange(BLOCK)[None, None, :]
    place = np.arange(16)[None, :, None] * 2 + np.arange(2)[:, None, None]
    source = np.where(inside < SHARD, place * SHARD + inside, -1).reshape(-1)
    pick_cols = jnp.asarray(np.arange(feats)[:, None] == source[None, :], bf16)

    both = jnp.stack([sent, partner])
    low, high = both[:, : count // 2], both[:, count // 2 : count]
    core_x = swapped(jnp.where(core == 0, high, low), "core")
    chip_x = between_chips(jnp.where(core == 0, low, high))

    states = jnp.concatenate([both[:, :count], in_order(core, chip_x, core_x, 1)], axis=1)
    states = times(states.reshape(4 * count, feats), pick_cols).astype(bf16)
    states = states.reshape(2, 2 * count, 2 * SIDE)

    own_all_p = swapped(own_sent, "core")
    other_main, own_all_p, _ = lax.optimization_barrier((other_main, own_all_p, partner))
    other_main_p = swapped(other_main, "core")
    scale = jnp.repeat(cosine_logit_scale, HEAD)[None, :]
    weights = (own_all, other_main, own_all_p, other_main_p)
    size = 2 * count
    grid = np.arange(size).reshape(2, 2, members, rows, HALF)
    order = one_hot(grid.transpose(3, 1, 0, 2, 4).reshape(-1), size)
    latent = front_latents(flags, states, weights, scale, order)
    tables, latent, own_all, own_all_p, other_main, other_main_p = lax.optimization_barrier(
        (both[:, count:], latent, own_all, own_all_p, other_main, other_main_p)
    )
    readers = [array[:, -16:].reshape(16 * 16, lanes) for array in (other_main, other_main_p)]
    obs = weighted_places(in_order(zh, tables[:1], tables[1:], 0), sensor_gridpoint.size)
    moved = exchanged(latent.reshape(16, size // 16, width)).reshape(size, width)

    grid = np.arange(size).reshape(16, 2, members, HALF)
    order = one_hot(grid.transpose(3, 1, 0, 2).reshape(-1), size)
    grid = np.arange(count).reshape(HALF, 16, members)
    back_order = one_hot(grid.transpose(1, 2, 0).reshape(-1), count)
    posterior = analysis(flags, moved, order, back_order, obs, *readers)
    back = exchanged(posterior.reshape(16, count // 16, width)).reshape(count, width)

    def strip(own, other):
        own, other = own[:, None, o_end : o_end + SHARD], other[:, None, o_end : o_end + SHARD]
        return in_order(zh, own, other, 1).reshape(feats, -1)

    grid = np.arange(count).reshape(rows, 2, members, HALF)
    order = one_hot(grid.transpose(2, 0, 1, 3).reshape(-1), count)
    result = decode(
        flags,
        back,
        order,
        strip(own_all, other_main),
        strip(own_all_p, other_main_p),
    )
    return result.reshape(members, rows, cols, feats)


def solution(mesh):
    fine = Mesh(
        np.asarray(mesh.devices).reshape(4, 4, 2, 8, 2), ("x", "y", "zh", "zl", "core")
    )
    return jax.shard_map(
        per_device,
        mesh=fine,
        in_specs=(
            P(MEM, None, TILE, None),
            P(MEM, None),
            P(None, MEM),
            P(None, MEM),
            P(None, MEM),
            P(),
            P(),
            P(MEM, TILE, None),
            P(MEM, TILE, None),
            P(MEM, TILE, None),
            P(MEM, TILE, None),
            P(MEM, TILE, None),
        ),
        out_specs=P(MEM, None, TILE, None),
        check_vma=False,
    )
```

```python
import functools

import numpy as np
import jax
import jax.numpy as jnp
from jax import lax
from jax.experimental import pallas as pl
from jax.experimental.pallas import tpu as pltpu
from jax.sharding import Mesh, PartitionSpec as P

PANE_SIDE = 8
HALF = PANE_SIDE // 2
NS_ITERS = 5
PLANE = ("x", "y")
MEM = ("x", "y", "zh")
TILE = ("zl", "core")
BLOCK = 40
SHARD = 35
SIDE = 16 * BLOCK
HEAD = 64
GROUP = 4 * HEAD
OWN = PANE_SIDE * HALF

eps_norm = 1e-05
normalizing_guard = 1e-06
bf16 = jnp.bfloat16
f32 = jnp.float32


def swapped(value, axis):
    return lax.ppermute(value, axis, [(0, 1), (1, 0)])


def shifted(value, by):
    return lax.ppermute(value, ("zh", "zl"), [(z, (z + by) % 16) for z in range(16)])


def crossed(value):
    pairs = [(z, 15 - z) for z in range(16)]
    return lax.ppermute(value, ("zh", "zl"), pairs)


def between_chips(value):
    pairs = [(2 * z, 2 * ((z - 1) % 8) + 1) for z in range(8)]
    return lax.ppermute(value, TILE, pairs + [(b, a) for a, b in pairs])


def copies_of(part):
    return lax.optimization_barrier(jnp.broadcast_to(part[None], (16,) + part.shape))


def exchanged(blocks):
    return lax.all_to_all(blocks, PLANE, split_axis=0, concat_axis=0, tiled=True)


def times(left, right):
    return jnp.dot(left, right, preferred_element_type=f32)


def times_t(left, right):
    return lax.dot_general(left, right, (((1,), (1,)), ((), ())), preferred_element_type=f32)


def normalized(values):
    center = values - jnp.mean(values, axis=-1, keepdims=True)
    spread = jnp.mean(center * center, axis=-1, keepdims=True)
    return center * lax.rsqrt(spread + eps_norm)


def in_order(flag, first, second, axis):
    low = jnp.where(flag == 0, first, second)
    high = jnp.where(flag == 0, second, first)
    return jnp.concatenate([low, high], axis=axis)


def halves(flag, value):
    width = value.shape[-1] // 2
    low, high = value[..., :width], value[..., width:]
    return jnp.where(flag == 0, low, high), jnp.where(flag == 0, high, low)


def two_parts(value):
    high = value.astype(bf16)
    return high, (value - high.astype(f32)).astype(bf16)


def three_parts(value):
    high = value.astype(bf16)
    rest = value - high.astype(f32)
    middle = rest.astype(bf16)
    return high, middle, (rest - middle.astype(f32)).astype(bf16)


def iota(shape, axis):
    return lax.broadcasted_iota(jnp.int32, shape, axis)


def one_hot(order, width):
    return jnp.asarray(np.asarray(order)[:, None] == np.arange(width)[None, :], bf16)


def front_kernel(
    flags,
    x_all,
    own_m,
    other_m,
    own_p,
    other_p,
    scale,
    order,
    latent_out,
    w_mine,
    w_part,
):
    core, zh = flags[0], flags[1]
    lanes = own_m.shape[2]
    lifts, outs = 6 * lanes // 32, 2 * lanes // 32
    front = lifts + BLOCK
    width = 2 * lanes

    for target, own, other in ((w_mine, own_m, other_m), (w_part, own_p, other_p)):
        for place in range(16):
            target[2 * lifts * place : 2 * lifts * (place + 1), :] = in_order(
                zh, own[place, :lifts, :], other[place, :lifts, :], 0
            )

    def embed(own, other):
        return times(x_own, own[:, lifts:front, :].reshape(SIDE, lanes)) + times(
            x_other, other[:, lifts:front, :].reshape(SIDE, lanes)
        )

    groups, count = x_all.shape[0], x_all.shape[1] // 2
    x = jnp.concatenate(
        [x_all[g, i * count : (i + 1) * count, :] for i in range(2) for g in range(groups)], axis=0
    )
    x_own, x_other = halves(zh, x)
    hidden = in_order(core, embed(own_m, other_m), embed(own_p, other_p), 1).astype(bf16)
    normed = normalized(hidden.astype(f32)).astype(bf16)
    n_mine, n_part = halves(core, normed)
    own_rows = groups * count

    same = (iota((GROUP, GROUP), 0) // HEAD) == (iota((GROUP, GROUP), 1) // HEAD)
    ones = same.astype(bf16)
    lane_head = iota((PANE_SIDE * PANE_SIDE, GROUP), 1) // HEAD

    def projected(left, right, start):
        rows = pl.ds(start, GROUP)
        return (times_t(left, w_mine[rows, :]) + times_t(right, w_part[rows, :])).astype(bf16)

    def unit(values):
        total = times(values * values, ones)
        values = values.astype(f32)
        return (values * lax.rsqrt(total + normalizing_guard)).astype(bf16)

    def diagonal(rows):
        zero = jnp.zeros_like(rows)
        return jnp.concatenate([jnp.where(lane_head == h, rows, zero) for h in range(4)], axis=0)

    def pane_rows(values, i):
        return jnp.concatenate(
            [values[i * OWN : (i + 1) * OWN], values[own_rows + i * OWN :][:OWN]], axis=0
        )

    panes = own_rows // OWN
    context = []
    for g in range(width // GROUP):
        at = g * GROUP
        query = unit(projected(n_mine[:own_rows], n_part[:own_rows], at))
        key_rows = unit(projected(n_mine, n_part, width + at))
        value_rows = projected(n_mine, n_part, 2 * width + at)
        scores = [
            times_t(query[i * OWN : (i + 1) * OWN], diagonal(pane_rows(key_rows, i)))
            for i in range(panes)
        ]
        weights = jnp.exp(jnp.concatenate(scores, axis=0) * scale[:, at : at + GROUP]).astype(bf16)
        total = times(weights, ones)
        mixed = [
            times(weights[i * OWN : (i + 1) * OWN], diagonal(pane_rows(value_rows, i)))
            for i in range(panes)
        ]
        context.append((jnp.concatenate(mixed, axis=0) / total).astype(bf16))
    c_mine, c_part = halves(core, jnp.concatenate(context, axis=1))

    def combiner(own, other):
        rows = [
            in_order(
                zh, own[place, front : front + outs, :], other[place, front : front + outs, :], 0
            )
            for place in range(16)
        ]
        return jnp.concatenate(rows, axis=0)

    mixed = times_t(c_mine, combiner(own_m, other_m)) + times_t(c_part, combiner(own_p, other_p))
    latent = normalized(hidden[:own_rows].astype(f32) + mixed).astype(bf16)
    latent_out[...] = times(order[...], latent).astype(bf16)


def front_latents(flags, states, weights, scale, order):
    lanes = weights[0].shape[2]
    vmem = pl.BlockSpec(memory_space=pltpu.VMEM)
    return pl.pallas_call(
        front_kernel,
        in_specs=[pl.BlockSpec(memory_space=pltpu.SMEM)] + [vmem] * (3 + len(weights)),
        out_specs=vmem,
        out_shape=jax.ShapeDtypeStruct((order.shape[0], 2 * lanes), bf16),
        scratch_shapes=[pltpu.VMEM((6 * lanes, lanes), bf16)] * 2,
        compiler_params=pltpu.CompilerParams(vmem_limit_bytes=16 * 1024 * 1024),
        name="front",
    )(flags, states, *weights, scale, order)


def prepare_kernel(x, order, grid, domain, channel, reading, noise, packed):
    count = x.shape[0]
    packed[:count, :] = times(order[...], x[...]).astype(bf16)
    table = [grid[...].astype(f32), domain[...].astype(f32), channel[...].astype(f32)]
    table = [t.astype(bf16) for t in table]
    table += list(three_parts(reading[...])) + list(three_parts(noise[...]))
    table = [t.astype(f32) for t in table]
    rest = jnp.zeros((1, packed.shape[1] - 3 * table[0].shape[1]), f32)
    table = [jnp.concatenate(table[3 * i : 3 * i + 3] + [rest], axis=1) for i in range(3)]
    table.append(jnp.zeros((5, packed.shape[1]), f32))
    packed[count:, :] = jnp.concatenate(table, axis=0).astype(bf16)


def prepare(x, order, *obs):
    vmem = pl.BlockSpec(memory_space=pltpu.VMEM)
    count, feats = x.shape
    return pl.pallas_call(
        prepare_kernel,
        in_specs=[vmem] * (2 + len(obs)),
        out_specs=vmem,
        out_shape=jax.ShapeDtypeStruct((count + 8, feats), bf16),
        name="prepare",
    )(x, order, *obs)


def product(left, right):
    l_high, l_low = two_parts(left)
    r_high, r_low = two_parts(right)
    return times(
        jnp.concatenate([l_high, l_high, l_low], axis=1),
        jnp.concatenate([r_high, r_low, r_high], axis=0),
    )


def product_t(left, right):
    l_high, l_low = two_parts(left)
    r_high, r_low = two_parts(right)
    return times_t(
        jnp.concatenate([l_high, l_high, l_low], axis=1),
        jnp.concatenate([r_high, r_low, r_high], axis=1),
    )


def analysis_kernel(flags, moved, order, back_order, obs, r_mine, r_part, posterior_out):
    latent = times(order[...], moved[...]).astype(bf16)
    members = latent.shape[0] // HALF
    l_mine, l_part = halves(flags[0], latent)

    seen = times_t(l_mine, r_mine[...]) + times_t(l_part, r_part[...])
    eye = (iota((members, members), 0) == iota((members, members), 1)).astype(f32)
    systems, drives = [], []
    for block in range(2):
        ens = [seen[(2 * block + t) * members : (2 * block + t + 1) * members] for t in range(2)]
        mean = [jnp.mean(e, axis=0, keepdims=True) for e in ens]
        pert = jnp.concatenate([e - m for e, m in zip(ens, mean)], axis=1)
        mean = jnp.concatenate(mean, axis=1)
        for r in range(2):
            weight = obs[block, r : r + 1, :]
            read = obs[block, 2 + r : 3 + r, :]
            gram = product_t(pert * weight, pert)
            drives.append(jnp.sum(pert * (read - weight * mean), axis=1, keepdims=True))
            systems.append(eye + gram / (members - 1.0))
    bounds = [
        jnp.max(jnp.sum(jnp.abs(s), axis=1, keepdims=True), axis=0, keepdims=True) for s in systems
    ]
    iterates = [s / b for s, b in zip(systems, bounds)]
    factors = [1.5 * eye - 0.5 * y for y in iterates]
    iterates = [product(y, f) for y, f in zip(iterates, factors)]
    roots = factors
    for step in range(1, NS_ITERS):
        factors = [1.5 * eye - 0.5 * product(z, y) for z, y in zip(roots, iterates)]
        if step + 1 < NS_ITERS:
            iterates = [product(y, f) for y, f in zip(iterates, factors)]
        roots = [product(f, z) for f, z in zip(factors, roots)]
    results = []
    for region in range(2 * 2):
        root = roots[region] * lax.rsqrt(bounds[region])
        inner = jnp.sum(root * drives[region], axis=0, keepdims=True)
        mean_weight = jnp.sum(root * inner, axis=1, keepdims=True) / (members - 1.0)
        transform = root + mean_weight
        own_t = transform[:, : members // 2].T
        values = latent[region * members : (region + 1) * members]
        center = jnp.mean(values.astype(f32), axis=0, keepdims=True)
        high, middle, low = three_parts(own_t)
        left = jnp.concatenate([high, middle, low], axis=1)
        moved_part = times(left, jnp.concatenate([values] * 3, axis=0))
        share = 1.0 - jnp.sum(own_t, axis=1, keepdims=True)
        results.append((moved_part + share * center).astype(bf16))
    posterior = jnp.concatenate(results, axis=0)
    posterior_out[...] = times(back_order[...], posterior).astype(bf16)


def analysis(flags, moved, order, back_order, obs, r_mine, r_part):
    vmem = pl.BlockSpec(memory_space=pltpu.VMEM)
    return pl.pallas_call(
        analysis_kernel,
        in_specs=[pl.BlockSpec(memory_space=pltpu.SMEM)] + [vmem] * 6,
        out_specs=vmem,
        out_shape=jax.ShapeDtypeStruct((back_order.shape[0], moved.shape[1]), bf16),
        compiler_params=pltpu.CompilerParams(vmem_limit_bytes=12 * 1024 * 1024),
        name="analysis",
    )(flags, moved, order, back_order, obs, r_mine, r_part)


def decode_kernel(flags, parts, order, d_mine, d_part, out):
    b_mine, b_part = halves(flags[0], times(order[...], parts[...]).astype(bf16))
    out[...] = (times_t(b_mine, d_mine[...]) + times_t(b_part, d_part[...])).astype(bf16)


def decode(flags, parts, order, d_mine, d_part):
    vmem = pl.BlockSpec(memory_space=pltpu.VMEM)
    return pl.pallas_call(
        decode_kernel,
        in_specs=[pl.BlockSpec(memory_space=pltpu.SMEM)] + [vmem] * 4,
        out_specs=vmem,
        out_shape=jax.ShapeDtypeStruct((order.shape[0], d_mine.shape[0]), bf16),
        compiler_params=pltpu.CompilerParams(vmem_limit_bytes=12 * 1024 * 1024),
        name="decode",
    )(flags, parts, order, d_mine, d_part)


def weighted_places(table, count):
    table = table[:, :3, : 3 * count].astype(f32).reshape(2, 9, count)
    grid = table[:, 0].astype(jnp.int32)
    domain = table[:, 1].astype(jnp.int32)
    channel = table[:, 2].astype(jnp.int32)
    reading = table[:, 3] + (table[:, 4] + table[:, 5])
    noise = table[:, 6] + (table[:, 7] + table[:, 8])
    token = grid // 16
    distance = (token - domain).astype(f32)
    weight = jnp.exp(-0.5 * distance * distance) / (noise * noise)
    region = (domain[:, None, :] == jnp.arange(2, dtype=jnp.int32)[None, :, None]).astype(f32)
    weight = region * weight[:, None, :]
    left = jnp.concatenate([weight, weight * reading[:, None, :]], axis=1)
    place = grid * 16 + channel
    pick = (place[:, :, None] == jnp.arange(512, dtype=jnp.int32)[None, None, :]).astype(f32)
    return jnp.einsum("bcj,bjp->bcp", left, pick, precision=lax.Precision.HIGHEST)


def per_device(
    starting_ensemble,
    patch_lifting,
    query_keyvalue_lift,
    output_combiner,
    decoder_linear_map,
    cosine_logit_scale,
    sensor_variable_loadings,
    sensor_gridpoint,
    sensor_domain_index,
    sensor_channel_list,
    sensor_reading,
    sensor_noise_deviation,
):
    members, rows, cols, feats = starting_ensemble.shape
    width = patch_lifting.shape[1]
    core = lax.axis_index("core")
    zh = lax.axis_index("zh")
    flags = jnp.stack([core, zh]).astype(jnp.int32)

    fill = ((0, BLOCK - SHARD), (0, 0))
    packed = jnp.concatenate(
        [
            query_keyvalue_lift.T,
            jnp.pad(patch_lifting, fill),
            output_combiner.T,
            jnp.pad(decoder_linear_map.T, fill),
        ],
        axis=0,
    )
    mine, _ = halves(core, packed)
    lanes = mine.shape[1]
    front = query_keyvalue_lift.shape[1] + BLOCK
    o_end = front + output_combiner.shape[1]
    own_all = exchanged(copies_of(mine))

    count = members * rows * cols
    grid = np.arange(count).reshape(members, rows, 2, HALF)
    pick_rows = one_hot(grid.transpose(2, 0, 1, 3).reshape(-1), count)
    obs = (
        sensor_gridpoint,
        sensor_domain_index,
        sensor_channel_list,
        sensor_reading,
        sensor_noise_deviation,
    )
    sent = prepare(
        starting_ensemble.reshape(count, feats), pick_rows, *(o.reshape(1, -1) for o in obs)
    )
    sent, outgoing = lax.optimization_barrier((sent, mine))
    theirs = crossed(outgoing)
    middle = (count + 8) // 2
    up, down = shifted(sent[:middle], 4), shifted(sent[middle:], -4)

    decoder = in_order(zh, mine[o_end:], theirs[o_end:], 0)
    loadings = jnp.pad(
        sensor_variable_loadings.reshape(16, 2, SHARD), ((0, 0), (0, 0), (0, BLOCK - SHARD))
    ).reshape(16, 2 * BLOCK)
    readers = times(loadings, decoder).astype(bf16)
    copies, own_all = lax.optimization_barrier(
        (copies_of(jnp.concatenate([theirs, readers], axis=0)), own_all)
    )
    up, down, own_sent = lax.optimization_barrier((up, down, own_all))
    partner = jnp.concatenate([shifted(up, 4), shifted(down, -4)], axis=0)
    other_main = exchanged(copies)
    inside = np.arange(BLOCK)[None, None, :]
    place = np.arange(16)[None, :, None] * 2 + np.arange(2)[:, None, None]
    source = np.where(inside < SHARD, place * SHARD + inside, -1).reshape(-1)
    pick_cols = jnp.asarray(np.arange(feats)[:, None] == source[None, :], bf16)

    both = jnp.stack([sent, partner])
    low, high = both[:, : count // 2], both[:, count // 2 : count]
    core_x = swapped(jnp.where(core == 0, high, low), "core")
    chip_x = between_chips(jnp.where(core == 0, low, high))

    states = jnp.concatenate([both[:, :count], in_order(core, chip_x, core_x, 1)], axis=1)
    states = times(states.reshape(4 * count, feats), pick_cols).astype(bf16)
    states = states.reshape(2, 2 * count, 2 * SIDE)

    own_all_p = swapped(own_sent, "core")
    other_main, own_all_p, _ = lax.optimization_barrier((other_main, own_all_p, partner))
    other_main_p = swapped(other_main, "core")
    scale = jnp.repeat(cosine_logit_scale, HEAD)[None, :]
    weights = (own_all, other_main, own_all_p, other_main_p)
    size = 2 * count
    grid = np.arange(size).reshape(2, 2, members, rows, HALF)
    order = one_hot(grid.transpose(3, 1, 0, 2, 4).reshape(-1), size)
    latent = front_latents(flags, states, weights, scale, order)
    tables, latent, own_all, own_all_p, other_main, other_main_p = lax.optimization_barrier(
        (both[:, count:], latent, own_all, own_all_p, other_main, other_main_p)
    )
    readers = [array[:, -16:].reshape(16 * 16, lanes) for array in (other_main, other_main_p)]
    obs = weighted_places(in_order(zh, tables[:1], tables[1:], 0), sensor_gridpoint.size)
    moved = exchanged(latent.reshape(16, size // 16, width)).reshape(size, width)

    grid = np.arange(size).reshape(16, 2, members, HALF)
    order = one_hot(grid.transpose(3, 1, 0, 2).reshape(-1), size)
    grid = np.arange(count).reshape(HALF, 16, members)
    back_order = one_hot(grid.transpose(1, 2, 0).reshape(-1), count)
    posterior = analysis(flags, moved, order, back_order, obs, *readers)
    back = exchanged(posterior.reshape(16, count // 16, width)).reshape(count, width)

    def strip(own, other):
        own, other = own[:, None, o_end : o_end + SHARD], other[:, None, o_end : o_end + SHARD]
        return in_order(zh, own, other, 1).reshape(feats, -1)

    grid = np.arange(count).reshape(rows, 2, members, HALF)
    order = one_hot(grid.transpose(2, 0, 1, 3).reshape(-1), count)
    result = decode(
        flags,
        back,
        order,
        strip(own_all, other_main),
        strip(own_all_p, other_main_p),
    )
    return result.reshape(members, rows, cols, feats)


def solution(mesh):
    fine = Mesh(
        np.asarray(mesh.devices).reshape(4, 4, 2, 8, 2), ("x", "y", "zh", "zl", "core")
    )
    return jax.shard_map(
        per_device,
        mesh=fine,
        in_specs=(
            P(MEM, None, TILE, None),
            P(MEM, None),
            P(None, MEM),
            P(None, MEM),
            P(None, MEM),
            P(),
            P(),
            P(MEM, TILE, None),
            P(MEM, TILE, None),
            P(MEM, TILE, None),
            P(MEM, TILE, None),
            P(MEM, TILE, None),
        ),
        out_specs=P(MEM, None, TILE, None),
        check_vma=False,
    )
```

```python
import functools

import numpy as np
import jax
import jax.numpy as jnp
from jax import lax
from jax.experimental import pallas as pl
from jax.experimental.pallas import tpu as pltpu
from jax.sharding import Mesh, PartitionSpec as P

PANE_SIDE = 8
HALF = PANE_SIDE // 2
NS_ITERS = 5
PLANE = ("x", "y")
MEM = ("x", "y", "zh")
TILE = ("zl", "core")
BLOCK = 40
SHARD = 35
SIDE = 16 * BLOCK
HEAD = 64
GROUP = 4 * HEAD
OWN = PANE_SIDE * HALF

eps_norm = 1e-05
normalizing_guard = 1e-06
bf16 = jnp.bfloat16
f32 = jnp.float32


def swapped(value, axis):
    return lax.ppermute(value, axis, [(0, 1), (1, 0)])


def shifted(value, by):
    return lax.ppermute(value, ("zh", "zl"), [(z, (z + by) % 16) for z in range(16)])


def crossed(value):
    pairs = [(z, 15 - z) for z in range(16)]
    return lax.ppermute(value, ("zh", "zl"), pairs)


def between_chips(value):
    pairs = [(2 * z, 2 * ((z - 1) % 8) + 1) for z in range(8)]
    return lax.ppermute(value, TILE, pairs + [(b, a) for a, b in pairs])


def copies_of(part):
    return lax.optimization_barrier(jnp.broadcast_to(part[None], (16,) + part.shape))


def exchanged(blocks):
    return lax.all_to_all(blocks, PLANE, split_axis=0, concat_axis=0, tiled=True)


def times(left, right):
    return jnp.dot(left, right, preferred_element_type=f32)


def times_t(left, right):
    return lax.dot_general(left, right, (((1,), (1,)), ((), ())), preferred_element_type=f32)


def normalized(values):
    center = values - jnp.mean(values, axis=-1, keepdims=True)
    spread = jnp.mean(center * center, axis=-1, keepdims=True)
    return center * lax.rsqrt(spread + eps_norm)


def in_order(flag, first, second, axis):
    low = jnp.where(flag == 0, first, second)
    high = jnp.where(flag == 0, second, first)
    return jnp.concatenate([low, high], axis=axis)


def halves(flag, value):
    width = value.shape[-1] // 2
    low, high = value[..., :width], value[..., width:]
    return jnp.where(flag == 0, low, high), jnp.where(flag == 0, high, low)


def two_parts(value):
    high = value.astype(bf16)
    return high, (value - high.astype(f32)).astype(bf16)


def three_parts(value):
    high = value.astype(bf16)
    rest = value - high.astype(f32)
    middle = rest.astype(bf16)
    return high, middle, (rest - middle.astype(f32)).astype(bf16)


def iota(shape, axis):
    return lax.broadcasted_iota(jnp.int32, shape, axis)


def one_hot(order, width):
    return jnp.asarray(np.asarray(order)[:, None] == np.arange(width)[None, :], bf16)


def front_kernel(
    flags,
    x_all,
    own_m,
    other_m,
    own_p,
    other_p,
    scale,
    order,
    latent_out,
    w_mine,
    w_part,
):
    core, zh = flags[0], flags[1]
    lanes = own_m.shape[2]
    lifts, outs = 6 * lanes // 32, 2 * lanes // 32
    front = lifts + BLOCK
    width = 2 * lanes

    for target, own, other in ((w_mine, own_m, other_m), (w_part, own_p, other_p)):
        for place in range(16):
            target[2 * lifts * place : 2 * lifts * (place + 1), :] = in_order(
                zh, own[place, :lifts, :], other[place, :lifts, :], 0
            )

    def embed(own, other):
        return times(x_own, own[:, lifts:front, :].reshape(SIDE, lanes)) + times(
            x_other, other[:, lifts:front, :].reshape(SIDE, lanes)
        )

    groups, count = x_all.shape[0], x_all.shape[1] // 2
    x = jnp.concatenate(
        [x_all[g, i * count : (i + 1) * count, :] for i in range(2) for g in range(groups)], axis=0
    )
    x_own, x_other = halves(zh, x)
    hidden = in_order(core, embed(own_m, other_m), embed(own_p, other_p), 1).astype(bf16)
    normed = normalized(hidden.astype(f32)).astype(bf16)
    n_mine, n_part = halves(core, normed)
    own_rows = groups * count

    same = (iota((GROUP, GROUP), 0) // HEAD) == (iota((GROUP, GROUP), 1) // HEAD)
    ones = same.astype(bf16)
    lane_head = iota((PANE_SIDE * PANE_SIDE, GROUP), 1) // HEAD

    def projected(left, right, start):
        rows = pl.ds(start, GROUP)
        return (times_t(left, w_mine[rows, :]) + times_t(right, w_part[rows, :])).astype(bf16)

    def unit(values):
        total = times(values * values, ones)
        values = values.astype(f32)
        return (values * lax.rsqrt(total + normalizing_guard)).astype(bf16)

    def diagonal(rows):
        zero = jnp.zeros_like(rows)
        return jnp.concatenate([jnp.where(lane_head == h, rows, zero) for h in range(4)], axis=0)

    def pane_rows(values, i):
        return jnp.concatenate(
            [values[i * OWN : (i + 1) * OWN], values[own_rows + i * OWN :][:OWN]], axis=0
        )

    panes = own_rows // OWN
    context = []
    for g in range(width // GROUP):
        at = g * GROUP
        query = unit(projected(n_mine[:own_rows], n_part[:own_rows], at))
        key_rows = unit(projected(n_mine, n_part, width + at))
        value_rows = projected(n_mine, n_part, 2 * width + at)
        scores = [
            times_t(query[i * OWN : (i + 1) * OWN], diagonal(pane_rows(key_rows, i)))
            for i in range(panes)
        ]
        weights = jnp.exp(jnp.concatenate(scores, axis=0) * scale[:, at : at + GROUP]).astype(bf16)
        total = times(weights, ones)
        mixed = [
            times(weights[i * OWN : (i + 1) * OWN], diagonal(pane_rows(value_rows, i)))
            for i in range(panes)
        ]
        context.append((jnp.concatenate(mixed, axis=0) / total).astype(bf16))
    c_mine, c_part = halves(core, jnp.concatenate(context, axis=1))

    def combiner(own, other):
        rows = [
            in_order(
                zh, own[place, front : front + outs, :], other[place, front : front + outs, :], 0
            )
            for place in range(16)
        ]
        return jnp.concatenate(rows, axis=0)

    mixed = times_t(c_mine, combiner(own_m, other_m)) + times_t(c_part, combiner(own_p, other_p))
    latent = normalized(hidden[:own_rows].astype(f32) + mixed).astype(bf16)
    latent_out[...] = times(order[...], latent).astype(bf16)


def front_latents(flags, states, weights, scale, order):
    lanes = weights[0].shape[2]
    vmem = pl.BlockSpec(memory_space=pltpu.VMEM)
    return pl.pallas_call(
        front_kernel,
        in_specs=[pl.BlockSpec(memory_space=pltpu.SMEM)] + [vmem] * (3 + len(weights)),
        out_specs=vmem,
        out_shape=jax.ShapeDtypeStruct((order.shape[0], 2 * lanes), bf16),
        scratch_shapes=[pltpu.VMEM((6 * lanes, lanes), bf16)] * 2,
        compiler_params=pltpu.CompilerParams(vmem_limit_bytes=16 * 1024 * 1024),
        name="front",
    )(flags, states, *weights, scale, order)


def prepare_kernel(x, order, grid, domain, channel, reading, noise, packed):
    count = x.shape[0]
    packed[:count, :] = times(order[...], x[...]).astype(bf16)
    table = [grid[...].astype(f32), domain[...].astype(f32), channel[...].astype(f32)]
    table = [t.astype(bf16) for t in table]
    table += list(three_parts(reading[...])) + list(three_parts(noise[...]))
    table = [t.astype(f32) for t in table]
    rest = jnp.zeros((1, packed.shape[1] - 3 * table[0].shape[1]), f32)
    table = [jnp.concatenate(table[3 * i : 3 * i + 3] + [rest], axis=1) for i in range(3)]
    table.append(jnp.zeros((5, packed.shape[1]), f32))
    packed[count:, :] = jnp.concatenate(table, axis=0).astype(bf16)


def prepare(x, order, *obs):
    vmem = pl.BlockSpec(memory_space=pltpu.VMEM)
    count, feats = x.shape
    return pl.pallas_call(
        prepare_kernel,
        in_specs=[vmem] * (2 + len(obs)),
        out_specs=vmem,
        out_shape=jax.ShapeDtypeStruct((count + 8, feats), bf16),
        name="prepare",
    )(x, order, *obs)


def product(left, right):
    l_high, l_low = two_parts(left)
    r_high, r_low = two_parts(right)
    return times(
        jnp.concatenate([l_high, l_high, l_low], axis=1),
        jnp.concatenate([r_high, r_low, r_high], axis=0),
    )


def product_t(left, right):
    l_high, l_low = two_parts(left)
    r_high, r_low = two_parts(right)
    return times_t(
        jnp.concatenate([l_high, l_high, l_low], axis=1),
        jnp.concatenate([r_high, r_low, r_high], axis=1),
    )


def analysis_kernel(flags, moved, order, back_order, obs, r_mine, r_part, posterior_out):
    latent = times(order[...], moved[...]).astype(bf16)
    members = latent.shape[0] // HALF
    l_mine, l_part = halves(flags[0], latent)

    seen = times_t(l_mine, r_mine[...]) + times_t(l_part, r_part[...])
    eye = (iota((members, members), 0) == iota((members, members), 1)).astype(f32)
    systems, drives = [], []
    for block in range(2):
        ens = [seen[(2 * block + t) * members : (2 * block + t + 1) * members] for t in range(2)]
        mean = [jnp.mean(e, axis=0, keepdims=True) for e in ens]
        pert = jnp.concatenate([e - m for e, m in zip(ens, mean)], axis=1)
        mean = jnp.concatenate(mean, axis=1)
        for r in range(2):
            weight = obs[block, r : r + 1, :]
            read = obs[block, 2 + r : 3 + r, :]
            gram = product_t(pert * weight, pert)
            drives.append(jnp.sum(pert * (read - weight * mean), axis=1, keepdims=True))
            systems.append(eye + gram / (members - 1.0))
    bounds = [
        jnp.max(jnp.sum(jnp.abs(s), axis=1, keepdims=True), axis=0, keepdims=True) for s in systems
    ]
    iterates = [s / b for s, b in zip(systems, bounds)]
    factors = [1.5 * eye - 0.5 * y for y in iterates]
    iterates = [product(y, f) for y, f in zip(iterates, factors)]
    roots = factors
    for step in range(1, NS_ITERS):
        factors = [1.5 * eye - 0.5 * product(z, y) for z, y in zip(roots, iterates)]
        if step + 1 < NS_ITERS:
            iterates = [product(y, f) for y, f in zip(iterates, factors)]
        roots = [product(f, z) for f, z in zip(factors, roots)]
    results = []
    for region in range(2 * 2):
        root = roots[region] * lax.rsqrt(bounds[region])
        inner = jnp.sum(root * drives[region], axis=0, keepdims=True)
        mean_weight = jnp.sum(root * inner, axis=1, keepdims=True) / (members - 1.0)
        transform = root + mean_weight
        own_t = transform[:, : members // 2].T
        values = latent[region * members : (region + 1) * members]
        center = jnp.mean(values.astype(f32), axis=0, keepdims=True)
        high, middle, low = three_parts(own_t)
        left = jnp.concatenate([high, middle, low], axis=1)
        moved_part = times(left, jnp.concatenate([values] * 3, axis=0))
        share = 1.0 - jnp.sum(own_t, axis=1, keepdims=True)
        results.append((moved_part + share * center).astype(bf16))
    posterior = jnp.concatenate(results, axis=0)
    posterior_out[...] = times(back_order[...], posterior).astype(bf16)


def analysis(flags, moved, order, back_order, obs, r_mine, r_part):
    vmem = pl.BlockSpec(memory_space=pltpu.VMEM)
    return pl.pallas_call(
        analysis_kernel,
        in_specs=[pl.BlockSpec(memory_space=pltpu.SMEM)] + [vmem] * 6,
        out_specs=vmem,
        out_shape=jax.ShapeDtypeStruct((back_order.shape[0], moved.shape[1]), bf16),
        compiler_params=pltpu.CompilerParams(vmem_limit_bytes=12 * 1024 * 1024),
        name="analysis",
    )(flags, moved, order, back_order, obs, r_mine, r_part)


def decode_kernel(flags, parts, order, d_mine, d_part, out):
    b_mine, b_part = halves(flags[0], times(order[...], parts[...]).astype(bf16))
    out[...] = (times_t(b_mine, d_mine[...]) + times_t(b_part, d_part[...])).astype(bf16)


def decode(flags, parts, order, d_mine, d_part):
    vmem = pl.BlockSpec(memory_space=pltpu.VMEM)
    return pl.pallas_call(
        decode_kernel,
        in_specs=[pl.BlockSpec(memory_space=pltpu.SMEM)] + [vmem] * 4,
        out_specs=vmem,
        out_shape=jax.ShapeDtypeStruct((order.shape[0], d_mine.shape[0]), bf16),
        compiler_params=pltpu.CompilerParams(vmem_limit_bytes=12 * 1024 * 1024),
        name="decode",
    )(flags, parts, order, d_mine, d_part)


def weighted_places(table, count):
    table = table[:, :3, : 3 * count].astype(f32).reshape(2, 9, count)
    grid = table[:, 0].astype(jnp.int32)
    domain = table[:, 1].astype(jnp.int32)
    channel = table[:, 2].astype(jnp.int32)
    reading = table[:, 3] + (table[:, 4] + table[:, 5])
    noise = table[:, 6] + (table[:, 7] + table[:, 8])
    token = grid // 16
    distance = (token - domain).astype(f32)
    weight = jnp.exp(-0.5 * distance * distance) / (noise * noise)
    region = (domain[:, None, :] == jnp.arange(2, dtype=jnp.int32)[None, :, None]).astype(f32)
    weight = region * weight[:, None, :]
    left = jnp.concatenate([weight, weight * reading[:, None, :]], axis=1)
    place = grid * 16 + channel
    pick = (place[:, :, None] == jnp.arange(512, dtype=jnp.int32)[None, None, :]).astype(f32)
    return jnp.einsum("bcj,bjp->bcp", left, pick, precision=lax.Precision.HIGHEST)


def per_device(
    starting_ensemble,
    patch_lifting,
    query_keyvalue_lift,
    output_combiner,
    decoder_linear_map,
    cosine_logit_scale,
    sensor_variable_loadings,
    sensor_gridpoint,
    sensor_domain_index,
    sensor_channel_list,
    sensor_reading,
    sensor_noise_deviation,
):
    members, rows, cols, feats = starting_ensemble.shape
    width = patch_lifting.shape[1]
    core = lax.axis_index("core")
    zh = lax.axis_index("zh")
    flags = jnp.stack([core, zh]).astype(jnp.int32)

    fill = ((0, BLOCK - SHARD), (0, 0))
    packed = jnp.concatenate(
        [
            query_keyvalue_lift.T,
            jnp.pad(patch_lifting, fill),
            output_combiner.T,
            jnp.pad(decoder_linear_map.T, fill),
        ],
        axis=0,
    )
    mine, _ = halves(core, packed)
    lanes = mine.shape[1]
    front = query_keyvalue_lift.shape[1] + BLOCK
    o_end = front + output_combiner.shape[1]
    own_all = exchanged(copies_of(mine))

    count = members * rows * cols
    grid = np.arange(count).reshape(members, rows, 2, HALF)
    pick_rows = one_hot(grid.transpose(2, 0, 1, 3).reshape(-1), count)
    obs = (
        sensor_gridpoint,
        sensor_domain_index,
        sensor_channel_list,
        sensor_reading,
        sensor_noise_deviation,
    )
    sent = prepare(
        starting_ensemble.reshape(count, feats), pick_rows, *(o.reshape(1, -1) for o in obs)
    )
    sent, outgoing = lax.optimization_barrier((sent, mine))
    theirs = crossed(outgoing)
    middle = (count + 8) // 2
    up, down = shifted(sent[:middle], 4), shifted(sent[middle:], -4)

    decoder = in_order(zh, mine[o_end:], theirs[o_end:], 0)
    loadings = jnp.pad(
        sensor_variable_loadings.reshape(16, 2, SHARD), ((0, 0), (0, 0), (0, BLOCK - SHARD))
    ).reshape(16, 2 * BLOCK)
    readers = times(loadings, decoder).astype(bf16)
    copies, own_all = lax.optimization_barrier(
        (copies_of(jnp.concatenate([theirs, readers], axis=0)), own_all)
    )
    up, down, own_sent = lax.optimization_barrier((up, down, own_all))
    up = shifted(up, 4)
    partner = jnp.concatenate([up, shifted(down, -4)], axis=0)
    other_main = exchanged(copies)
    inside = np.arange(BLOCK)[None, None, :]
    place = np.arange(16)[None, :, None] * 2 + np.arange(2)[:, None, None]
    source = np.where(inside < SHARD, place * SHARD + inside, -1).reshape(-1)
    pick_cols = jnp.asarray(np.arange(feats)[:, None] == source[None, :], bf16)

    both = jnp.stack([sent, partner])
    low, high = both[:, : count // 2], both[:, count // 2 : count]
    core_x = swapped(jnp.where(core == 0, high, low), "core")
    chip_x = between_chips(jnp.where(core == 0, low, high))

    states = jnp.concatenate([both[:, :count], in_order(core, chip_x, core_x, 1)], axis=1)
    states = times(states.reshape(4 * count, feats), pick_cols).astype(bf16)
    states = states.reshape(2, 2 * count, 2 * SIDE)

    own_all_p = swapped(own_sent, "core")
    other_main, own_all_p, _ = lax.optimization_barrier((other_main, own_all_p, up))
    other_main_p = swapped(other_main, "core")
    scale = jnp.repeat(cosine_logit_scale, HEAD)[None, :]
    weights = (own_all, other_main, own_all_p, other_main_p)
    size = 2 * count
    grid = np.arange(size).reshape(2, 2, members, rows, HALF)
    order = one_hot(grid.transpose(3, 1, 0, 2, 4).reshape(-1), size)
    latent = front_latents(flags, states, weights, scale, order)
    tables, latent, own_all, own_all_p, other_main, other_main_p = lax.optimization_barrier(
        (both[:, count:], latent, own_all, own_all_p, other_main, other_main_p)
    )
    readers = [array[:, -16:].reshape(16 * 16, lanes) for array in (other_main, other_main_p)]
    obs = weighted_places(in_order(zh, tables[:1], tables[1:], 0), sensor_gridpoint.size)
    moved = exchanged(latent.reshape(16, size // 16, width)).reshape(size, width)

    grid = np.arange(size).reshape(16, 2, members, HALF)
    order = one_hot(grid.transpose(3, 1, 0, 2).reshape(-1), size)
    grid = np.arange(count).reshape(HALF, 16, members)
    back_order = one_hot(grid.transpose(1, 2, 0).reshape(-1), count)
    posterior = analysis(flags, moved, order, back_order, obs, *readers)
    back = exchanged(posterior.reshape(16, count // 16, width)).reshape(count, width)

    def strip(own, other):
        own, other = own[:, None, o_end : o_end + SHARD], other[:, None, o_end : o_end + SHARD]
        return in_order(zh, own, other, 1).reshape(feats, -1)

    grid = np.arange(count).reshape(rows, 2, members, HALF)
    order = one_hot(grid.transpose(2, 0, 1, 3).reshape(-1), count)
    result = decode(
        flags,
        back,
        order,
        strip(own_all, other_main),
        strip(own_all_p, other_main_p),
    )
    return result.reshape(members, rows, cols, feats)


def solution(mesh):
    fine = Mesh(
        np.asarray(mesh.devices).reshape(4, 4, 2, 8, 2), ("x", "y", "zh", "zl", "core")
    )
    return jax.shard_map(
        per_device,
        mesh=fine,
        in_specs=(
            P(MEM, None, TILE, None),
            P(MEM, None),
            P(None, MEM),
            P(None, MEM),
            P(None, MEM),
            P(),
            P(),
            P(MEM, TILE, None),
            P(MEM, TILE, None),
            P(MEM, TILE, None),
            P(MEM, TILE, None),
            P(MEM, TILE, None),
        ),
        out_specs=P(MEM, None, TILE, None),
        check_vma=False,
    )
```
